256 devices in a mesh: vocab: 64 (over y, z_hi, x), tok: 4 (over z_lo, core).
Axes of the slice: x: 4, y: 4, z: 8 (z_hi: 4, z_lo: 2; z = z_hi * 2 + z_lo), core: 2. Of those that a mesh axis runs over, the one named last changes fastest.
Arguments:
- hidden: bfloat16 [768, 3072], P('tok', 'vocab'), may hold values from -40 to 40
- hidden_tangent: bfloat16 [768, 3072], P('tok', 'vocab'), may hold values from -6 to 6
- head: bfloat16 [3072, 65536], P('tok', 'vocab'), may hold values from -2 to 2
- head_tangent: bfloat16 [3072, 65536], P('tok', 'vocab'), may hold values from -0.109375 to 0.109375
- ref_logits: bfloat16 [768, 65536], P('tok', 'vocab'), may hold values from -240 to 240
- actions: int32 [768], P('tok'), may hold values from 0 to 65535
- valid: int32 [768], P('tok'), may hold values 0 or 1
Outputs:
- head_product: bfloat16 [3072, 65536], P('tok', 'vocab')
- hidden_product: bfloat16 [768, 3072], P('tok', 'vocab')
- penalty: float32 [768], P('tok')
- action_logprob: float32 [768], P('tok')
The draws below stay inside these ranges and needn't reach their ends.
All inputs are finite; a program needn't handle non-finite values. No bound on the sum of `valid` on one device may be relied on, other than what follows from the above.
Results may differ from the reference program's by a relative error of at most 0.008.
Values may be sent and summed in bfloat16 or wider, within the bound.
A program may use at most 64 MiB of HBM per device.

```python
import math
import jax
import jax.numpy as jnp
import numpy as np
from jax import lax

D = 3072
TOK_DEV = 192
V = 65536
TOKENS = 768
N_TOK = 4


def draw_hidden(key, part):
    key = jax.random.fold_in(key, 11)
    values = jax.random.truncated_normal(key, -5.0, 5.0, (TOKENS, D), jnp.float32)
    return values.astype(jnp.bfloat16)


def draw_head(key, part):
    key = jax.random.fold_in(key, 12)
    values = jax.random.truncated_normal(key, -5.0, 5.0, (D, V), jnp.float32) * (3.0 / jnp.sqrt(jnp.float32(D)))
    return values.astype(jnp.bfloat16)


def draw_ref_logits(key, part):
    key = jax.random.fold_in(key, 13)
    values = 3.0 * jax.random.truncated_normal(key, -5.0, 5.0, (TOKENS, V), jnp.float32)
    return values.astype(jnp.bfloat16)


def place_ends(result, stream_key, low, high):
    dims = result.shape
    place = [jax.random.randint(jax.random.fold_in(stream_key, axis), (), 0, dims[axis]) for axis in range(len(dims))]
    result = result.at[tuple(place)].set(low)
    longest = dims.index(max(dims))
    place[longest] = (place[longest] + 1) % dims[longest]
    return result.at[tuple(place)].set(high)


def steps_of(key, dims, pieces, smallest, top_value):
    gain, own = 1.0, jax.random.fold_in(key, 6)
    for axis_at, shards_of in pieces:
        steps = jnp.exp(jax.random.uniform(jax.random.fold_in(own, axis_at), (shards_of,), jnp.float32, smallest / len(pieces), top_value / len(pieces)))
        gain = gain * jnp.repeat(steps, dims[axis_at] // shards_of).reshape([-1 if axis == axis_at else 1 for axis in range(len(dims))])
    return gain


def rank_bounds(count, skew):
    portions = [(1 << 20) // math.isqrt(standing ** skew) + 1 for standing in range(1, count + 1)]
    spread = 1 + sum(portions) // (1 << 30)
    return np.cumsum(np.array([max(1, weight // spread) for weight in portions]))


def ranked_ids(stream_key, dims, count, lean):
    table = rank_bounds(count, lean)
    pick = jax.random.randint(jax.random.fold_in(stream_key, 1), dims, 0, int(table[count - 1]))
    rank = jnp.searchsorted(jnp.asarray(table, jnp.int32), pick, side="right")
    return jax.random.permutation(jax.random.fold_in(stream_key, 2), count)[rank].astype(jnp.int32)


def centred(rng, extent, spread, limit, split=(), held_as=jnp.bfloat16):
    level = steps_of(rng, extent, split, -0.22, 0.18) if split else 1.0
    values = jax.random.normal(rng, extent, jnp.float32) * spread * level
    return jnp.minimum(jnp.maximum(values, -limit), limit).astype(held_as)


def setup_inputs(seed: int = 0) -> dict:
    key_of = jax.random.split(jax.random.key(seed), 8)
    hidden = draw_hidden(jax.random.fold_in(key_of[7], 71), 0)
    hidden_tangent = centred(key_of[1], (TOKENS, D), 1.0, 6.0, ((0, 4), (1, 64)))
    head = draw_head(jax.random.fold_in(key_of[7], 71), 0)
    head_tangent = centred(key_of[3], (D, V), D ** -0.5, 0.109375, ((0, 4), (1, 64)))
    ref_logits = draw_ref_logits(jax.random.fold_in(key_of[7], 71), 0)
    actions = place_ends(ranked_ids(key_of[5], (TOKENS,), V, 2), jax.random.fold_in(key_of[5], 3), 0, V - 1).astype(jnp.int32)
    valid = place_ends((jax.random.randint(key_of[6], (TOKENS,), 0, 4) < 3).astype(jnp.int32), jax.random.fold_in(key_of[6], 1), 0, 1)
    return dict(hidden=hidden, hidden_tangent=hidden_tangent, head=head, head_tangent=head_tangent, ref_logits=ref_logits, actions=actions, valid=valid)


def lane(head, head_tangent, carry, block):
    hidden, hidden_tangent, ref_logits, actions, valid = block
    logits = jnp.dot(hidden, head, preferred_element_type=jnp.float32)
    tangent = jnp.dot(hidden, head_tangent, preferred_element_type=jnp.float32) + jnp.dot(hidden_tangent, head, preferred_element_type=jnp.float32)
    top = jnp.max(logits, 1)
    log_total = top + jnp.log(jnp.sum(jnp.exp(logits - top[:, None]), 1))
    ref_float = ref_logits.astype(jnp.float32)
    ref_top = jnp.max(ref_float, 1)
    ref_total = ref_top + jnp.log(jnp.sum(jnp.exp(ref_float - ref_top[:, None]), 1))
    probs = jnp.exp(logits - log_total[:, None])
    refp = jnp.exp(ref_float - ref_total[:, None])
    mean_tangent = jnp.sum(probs * tangent, 1)
    valid_float = valid.astype(jnp.float32)
    penalty = valid_float * (jnp.sum(refp * (ref_float - logits), 1) - ref_total + log_total)
    picked = jnp.take_along_axis(logits, actions.astype(jnp.int32)[:, None], 1)[:, 0]
    action_logprob = picked - log_total
    fisher = (valid_float[:, None] * probs * (tangent - mean_tangent[:, None])).astype(jnp.bfloat16)
    carry = carry + lax.dot_general(hidden, fisher, (((0,), (0,)), ((), ())), preferred_element_type=jnp.float32)
    hidden_product = lax.dot_general(fisher, head, (((1,), (1,)), ((), ())), preferred_element_type=jnp.float32).astype(jnp.bfloat16)
    return carry, (hidden_product, penalty, action_logprob)


def reference(hidden, hidden_tangent, head, head_tangent, ref_logits, actions, valid):
    blocks = (hidden.reshape(N_TOK, TOK_DEV, D), hidden_tangent.reshape(N_TOK, TOK_DEV, D),
              ref_logits.reshape(N_TOK, TOK_DEV, V), actions.reshape(N_TOK, TOK_DEV), valid.reshape(N_TOK, TOK_DEV))
    start = jnp.zeros((D, V), jnp.float32)
    total, outs = lax.scan(lambda carry, block: lane(head, head_tangent, carry, block), start, blocks)
    hidden_product, penalty, action_logprob = outs
    return (total.astype(jnp.bfloat16), hidden_product.reshape(TOKENS, D),
            penalty.reshape(TOKENS), action_logprob.reshape(TOKENS))
```

```python
import functools

import jax
import jax.numpy as jnp
from jax import lax
from jax.experimental import pallas as pl
from jax.experimental.pallas import tpu as pltpu
from jax.sharding import PartitionSpec as P

F32 = jnp.float32
BF16 = jnp.bfloat16
MESH = pl.DeviceIdType.MESH
ORDER = (3, 2, 1, 0)


def low_lanes(rows):
    return lax.broadcasted_iota(jnp.int32, (rows, 128), 1) < 64


def swap_halves(value):
    return pltpu.roll(value, 64, 1)


def merge(stats):
    tops = [s[0:1] for s in stats]
    ref_tops = [s[3:4] for s in stats]
    top = functools.reduce(jnp.maximum, tops)
    ref_top = functools.reduce(jnp.maximum, ref_tops)
    scale = [jnp.exp(a - top) for a in tops]
    ref_scale = [jnp.exp(a - ref_top) for a in ref_tops]
    n = range(len(stats))
    return (
        top,
        sum(stats[i][1:2] * scale[i] for i in n),
        sum(stats[i][2:3] * scale[i] for i in n),
        ref_top,
        sum(stats[i][4:5] * ref_scale[i] for i in n),
        sum(stats[i][5:6] * ref_scale[i] for i in n),
        sum(stats[i][6:7] for i in n),
    )


def kernel(
    s_ref, head_ref, ht_ref, ref_ref, act_ref, val_ref,
    hp_ref, hid_ref, tok_ref,
    head_t, ht_t, ref_t, ybuf, hbuf, hun, tun,
    out3, in3, out1, in1, xl, xt, rl, rt, lg, tg,
    sst, sbuf, fbuf, fun, ep,
    e1s, e1r, e2s, e2r, zsend, zrecv, ysend, yrecv,
    ya_s, ya_r, za_s, za_r, xa_s, xa_r, b3_s, b3_r, b1_s, b1_r, bl_s, bl_r, bt_s, bt_r,
    c_s, c_r, d1_s, d1_r, d2_s, d2_r, d3_s, d3_r, e1_s, e1_q, e2_s, e2_q, ez_s, ez_r, ey_s, ey_r,
):
    v = lax.axis_index("vocab")
    t = lax.axis_index("tok")
    y, zh, x = v // 16, (v // 4) % 4, v % 4
    zl, c = t // 2, t % 2

    def at_x(d):
        return (v - x + (x + d) % 4, t)

    def at_y(d):
        return ((y + d) % 4 * 16 + zh * 4 + x, t)

    def tok_of(r):
        return (zl + r // 2) % 2 * 2 + (c + r % 2) % 2

    def at_z(r, d):
        return (y * 16 + (zh + d) % 4 * 4 + x, tok_of(r))

    def send(src, dst, ssem, rsem, device):
        return pltpu.make_async_remote_copy(
            src_ref=src, dst_ref=dst, send_sem=ssem, recv_sem=rsem,
            device_id=device, device_id_type=MESH,
        )

    barrier = pltpu.get_barrier_semaphore()
    column = [(r, d) for r in ORDER for d in range(4) if (r, d) != (0, 0)]
    peers = [at_x(d) for d in (1, 2, 3)] + [at_y(d) for d in (1, 2, 3)] + [at_z(r, d) for r, d in column]
    for peer in peers:
        pl.semaphore_signal(barrier, inc=1, device_id=peer, device_id_type=MESH)
    pl.semaphore_wait(barrier, len(peers))

    y_copies = [send(s_ref, ybuf.at[y], ya_s.at[d], ya_r.at[d], at_y(d + 1)) for d in range(3)]
    for copy in y_copies:
        copy.start()
    ybuf[y] = s_ref[...]
    for copy in y_copies:
        copy.wait_recv()

    z_copies = {
        (r, d): send(ybuf.at[tok_of(r)], hbuf.at[r, zh, x], za_s.at[r * 4 + d], za_r.at[r * 4 + d], at_z(r, d))
        for r, d in column
    }
    for key in column:
        z_copies[key].start()
    hbuf[0, zh, x] = ybuf[t]

    for j in range(4):
        for half in range(2):
            cols = slice(half * 512 + j * 128, half * 512 + j * 128 + 128)
            head_t[j, half * 128 : half * 128 + 128] = head_ref[:, cols].T
            ht_t[j, half * 128 : half * 128 + 128] = ht_ref[:, cols].T
            ref_t[j, half * 128 : half * 128 + 128] = ref_ref[0:128, cols].astype(F32).T
        a, b = slice(j * 128, j * 128 + 128), slice(512 + j * 128, 512 + j * 128 + 128)
        tails = jnp.concatenate([ref_ref[128:192, a].astype(F32), ref_ref[128:192, b].astype(F32)], axis=0)
        ref_t[j, 256:384] = tails.T

    left_x, right_x = (x + 3) % 4, (x + 1) % 4
    x_first, x_second = {}, {}
    for r in ORDER:
        own = hbuf.at[r, :, x]
        x_first[r] = (
            send(own, own, xa_s.at[r, 0], xa_r.at[r, 0], at_x(1)),
            send(own, own, xa_s.at[r, 1], xa_r.at[r, 1], at_x(3)),
        )
        from_left = hbuf.at[r, 0:2, left_x]
        from_right = hbuf.at[r, 2:4, right_x]
        x_second[r] = (
            send(from_left, from_left, xa_s.at[r, 2], xa_r.at[r, 2], at_x(1)),
            send(from_right, from_right, xa_s.at[r, 3], xa_r.at[r, 3], at_x(3)),
        )

    def x_start(r):
        for d in range(4):
            if (r, d) != (0, 0):
                z_copies[r, d].wait_recv()
        for copy in x_first[r]:
            copy.start()

    def x_forward(r):
        for first, second in zip(x_first[r], x_second[r]):
            first.wait_recv()
            second.start()

    def unpack(r):
        for copy in x_second[r]:
            copy.wait_recv()
        low = low_lanes(768)
        block = hbuf[r].reshape(768, 384)
        tails = block[:, 256:384].astype(F32)
        other = swap_halves(tails)
        hun[:, r * 256 : r * 256 + 128] = block[:, 0:128]
        hun[:, r * 256 + 128 : r * 256 + 256] = jnp.where(low, tails, other).astype(BF16)
        tun[:, 0:128] = block[:, 128:256]
        tun[:, 128:256] = jnp.where(low, other, tails).astype(BF16)

    low128 = low_lanes(128)

    def pack(value):
        tail = jnp.where(low128, value[0:128, 128:256], value[128:256, 128:256])
        return value[:, 0:128], tail

    def partial(r, j):
        h = hun[:, r * 256 : r * 256 + 256]
        logits = jnp.dot(head_t[j], h, preferred_element_type=F32)
        tangent = jnp.dot(head_t[j], tun[...], preferred_element_type=F32) + jnp.dot(
            ht_t[j], h, preferred_element_type=F32
        )
        return pack(logits) + pack(tangent)

    sibling = (v, tok_of(1))
    across = (v, tok_of(2))

    def to_sibling(j, out, into, ssem, rsem):
        return send(out.at[j], into.at[j], ssem.at[j], rsem.at[j], sibling)

    def cross_l(j):
        return send(xl.at[j], rl.at[j], bl_s.at[j], bl_r.at[j], across)

    def cross_t(j):
        return send(xt.at[j], rt.at[j], bt_s.at[j], bt_r.at[j], across)

    def give(r, out, into, ssem, rsem):
        @pl.loop(0, 4)
        def _(j):
            lm, lt, tm, tt = partial(r, j)
            out[j, 0, 0:256] = lm
            out[j, 0, 256:384] = lt
            out[j, 1, 0:256] = tm
            out[j, 1, 256:384] = tt
            to_sibling(j, out, into, ssem, rsem).start()

    x_start(3)
    x_start(2)
    x_forward(3)
    x_start(1)
    x_forward(2)
    x_start(0)
    unpack(3)
    give(3, out3, in3, b3_s, b3_r)
    x_forward(1)
    unpack(2)

    @pl.loop(0, 4)
    def _(j):
        lm, lt, tm, tt = partial(2, j)
        to_sibling(j, out3, in3, b3_s, b3_r).wait_recv()
        xl[j, 0:256] = lm + in3[j, 0, 0:256]
        xl[j, 256:384] = lt + in3[j, 0, 256:384]
        xt[j, 0:256] = (tm + in3[j, 1, 0:256]).astype(BF16)
        xt[j, 256:384] = (tt + in3[j, 1, 256:384]).astype(BF16)
        cross_l(j).start()
        cross_t(j).start()

    x_forward(0)
    unpack(1)
    give(1, out1, in1, b1_s, b1_r)
    unpack(0)

    @pl.loop(0, 4)
    def _(j):
        lm, lt, tm, tt = partial(0, j)
        to_sibling(j, out1, in1, b1_s, b1_r).wait_recv()
        lg[j, 0:256] = lm + in1[j, 0, 0:256]
        lg[j, 256:384] = lt + in1[j, 0, 256:384]
        tg[j, 0:256] = tm + in1[j, 1, 0:256]
        tg[j, 256:384] = tt + in1[j, 1, 256:384]

    lowest = jnp.full((1, 128), -jnp.inf, F32)

    def maxima(j, carry):
        top_m, top_t, ref_m, ref_tl = carry
        cross_l(j).wait_recv()
        cross_t(j).wait_recv()
        logits = lg[j] + rl[j]
        lg[j] = logits
        tg[j] = tg[j] + rt[j].astype(F32)
        ref = ref_t[j]
        return (
            jnp.maximum(top_m, jnp.max(logits[0:256], 0, keepdims=True)),
            jnp.maximum(top_t, jnp.max(logits[256:384], 0, keepdims=True)),
            jnp.maximum(ref_m, jnp.max(ref[0:256], 0, keepdims=True)),
            jnp.maximum(ref_tl, jnp.max(ref[256:384], 0, keepdims=True)),
        )

    top_m, top_t, ref_m, ref_tl = lax.fori_loop(0, 4, maxima, (lowest,) * 4)
    top_t = jnp.maximum(top_t, swap_halves(top_t))
    ref_tl = jnp.maximum(ref_tl, swap_halves(ref_tl))

    row = lax.broadcasted_iota(jnp.int32, (256, 128), 0)
    main_col = jnp.where(row < 128, row, row + 384)
    tail_row = lax.broadcasted_iota(jnp.int32, (128, 128), 0)
    tail_col = jnp.where(low128, tail_row, tail_row + 512)
    wanted_m = act_ref[:, 0:128] - v * 1024
    wanted_t = act_ref[:, 128:256] - v * 1024

    def sums(j, carry):
        def part(logits, tangent, ref, top, ref_top, col, wanted, old):
            weights = jnp.exp(logits - top)
            ref_weights = jnp.exp(ref - ref_top)
            picked = jnp.where(col + j * 128 == wanted, logits, 0.0)
            new = (weights, weights * tangent, ref_weights, ref_weights * (ref - logits), picked)
            return tuple(o + jnp.sum(n, 0, keepdims=True) for o, n in zip(old, new))

        main = part(lg[j, 0:256], tg[j, 0:256], ref_t[j, 0:256], top_m, ref_m, main_col, wanted_m, carry[0:5])
        tail = part(
            lg[j, 256:384], tg[j, 256:384], ref_t[j, 256:384], top_t, ref_tl, tail_col, wanted_t, carry[5:10]
        )
        return main + tail

    found = lax.fori_loop(0, 4, sums, (jnp.zeros((1, 128), F32),) * 10)
    tails = [value + swap_halves(value) for value in found[5:10]]
    rows_m = [top_m, found[0], found[1], ref_m, found[2], found[3], found[4]]
    rows_t = [top_t, tails[0], tails[1], ref_tl, tails[2], tails[3], tails[4]]
    for i in range(7):
        sst[0, i : i + 1, 0:128] = rows_m[i]
        sst[0, i : i + 1, 128:256] = rows_t[i]
    sst[:, 7:8] = jnp.zeros((3, 1, 256), F32)

    c_copies = []
    for k, place in enumerate((at_x, at_y, lambda d: at_z(0, d))):
        now = [send(sst.at[k], sbuf.at[k, d], c_s.at[k, d], c_r.at[k, d], place(d + 1)) for d in range(3)]
        for copy in now:
            copy.start()
        for copy in now:
            copy.wait_recv()
        merged = merge([sst[k], sbuf[k, 0], sbuf[k, 1], sbuf[k, 2]])
        if k < 2:
            for i in range(7):
                sst[k + 1, i : i + 1] = merged[i]
        c_copies += now

    top, total, moment, ref_top, ref_sum, cross, chosen = merged
    log_total = top + jnp.log(total)
    mean_tangent = moment / total
    valid = val_ref[...].astype(F32)
    tok_ref[0:1] = valid * (cross / ref_sum - (ref_top + jnp.log(ref_sum)) + log_total)
    tok_ref[1:2] = chosen - log_total

    def d_sibling(j):
        return send(fbuf.at[0, j], fbuf.at[1, j], d1_s.at[j], d1_r.at[j], sibling)

    def d_across(j):
        return send(fbuf.at[0, j], fbuf.at[2, j], d2_s.at[j], d2_r.at[j], across)

    def d_relay(j):
        return send(fbuf.at[2, j], fbuf.at[3, j], d3_s.at[j], d3_r.at[j], sibling)

    @pl.loop(0, 4)
    def _(j):
        def part(rows, lanes):
            return (
                valid[:, lanes] * jnp.exp(lg[j, rows] - log_total[:, lanes]) * (tg[j, rows] - mean_tangent[:, lanes])
            ).astype(BF16)

        fbuf[0, j, 0:256] = part(slice(0, 256), slice(0, 128))
        fbuf[0, j, 256:384] = part(slice(256, 384), slice(128, 256))
        d_across(j).start()
        d_sibling(j).start()

    def unpack_fisher(r):
        for j in range(4):
            block = fbuf[r, j]
            tail = block[256:384]
            zero = jnp.zeros_like(tail)
            for half in range(2):
                rows = slice(half * 512 + j * 128, half * 512 + j * 128 + 128)
                fun[rows, r * 256 : r * 256 + 128] = block[half * 128 : half * 128 + 128]
                fun[rows, r * 256 + 128 : r * 256 + 256] = (
                    jnp.where(low128, tail, zero) if half == 0 else jnp.where(low128, zero, tail)
                )

    low192 = low_lanes(192)

    def hidden_part(p):
        @pl.loop(0, 4)
        def _(k):
            rows = pl.ds(pl.multiple_of(k * 192, 192), 192)
            part = jnp.dot(head_ref[rows, :], fun[:, p * 512 : p * 512 + 512], preferred_element_type=F32)
            even, odd = part[:, 128:256], part[:, 384:512]
            tail = jnp.where(low192, even + swap_halves(even), odd + swap_halves(odd))
            ep[p, k, :, :, 0:128] = part[:, 0:128].reshape(4, 48, 128)
            ep[p, k, :, :, 128:256] = part[:, 256:384].reshape(4, 48, 128)
            ep[p, k, :, :, 256:384] = tail.reshape(4, 48, 128)

    e1, e2 = {}, {}
    for p in range(2):
        for side, d in ((0, 1), (1, 3)):
            e1[p, side] = send(e1s.at[p, side], e1r.at[p, side], e1_s.at[p, side], e1_q.at[p, side], at_x(d))
            e2[p, side] = send(e2s.at[p, side], e2r.at[p, side], e2_s.at[p, side], e2_q.at[p, side], at_x(d))

    def e_first(p):
        far = (x + 2) % 4
        e1s[p, 0] = ep[p, 0:2, far].astype(BF16)
        e1s[p, 1] = ep[p, 2:4, far].astype(BF16)
        e1[p, 0].start()
        e1[p, 1].start()

    def e_second(p):
        e2s[p, 0, 2:4] = ep[p, 2:4, right_x].astype(BF16)
        e2s[p, 1, 0:2] = ep[p, 0:2, left_x].astype(BF16)
        e1[p, 0].wait_recv()
        e2s[p, 0, 0:2] = (ep[p, 0:2, right_x] + e1r[p, 0].astype(F32)).astype(BF16)
        e2[p, 0].start()
        e1[p, 1].wait_recv()
        e2s[p, 1, 2:4] = (ep[p, 2:4, left_x] + e1r[p, 1].astype(F32)).astype(BF16)
        e2[p, 1].start()

    ez = {
        (r, d): send(
            zsend.at[r, (zh + d) % 4], zrecv.at[r, d], ez_s.at[r * 4 + d], ez_r.at[r * 4 + d], at_z(r, d)
        )
        for r, d in column
    }

    def e_third(p):
        e2[p, 0].wait_recv()
        e2[p, 1].wait_recv()
        total_x = (ep[p, :, x] + e2r[p, 0].astype(F32) + e2r[p, 1].astype(F32)).astype(BF16)
        for odd in range(2):
            zsend[p * 2 + odd, :, :, 0:128] = total_x[:, :, odd * 128 : odd * 128 + 128]
            zsend[p * 2 + odd, :, :, 128:256] = total_x[:, :, 256:384]
        for r in (p * 2 + 1, p * 2):
            for d in range(4):
                if (r, d) != (0, 0):
                    ez[r, d].start()

    unpack_fisher(0)
    for j in range(4):
        d_sibling(j).wait_recv()
    unpack_fisher(1)
    for j in range(2):
        d_across(j).wait_recv()
        d_relay(j).start()
    hidden_part(0)
    e_first(0)
    for j in range(2, 4):
        d_across(j).wait_recv()
        d_relay(j).start()
    unpack_fisher(2)
    for j in range(4):
        d_relay(j).wait_recv()
    unpack_fisher(3)
    hidden_part(1)
    e_first(1)
    e_second(0)
    e_second(1)

    @pl.loop(0, 3)
    def _(k):
        rows = pl.ds(pl.multiple_of(k * 256, 256), 256)
        hp_ref[rows, :] = lax.dot_general(
            hun[rows, :], fun[...], (((1,), (1,)), ((), ())), preferred_element_type=F32
        ).astype(BF16)

    e_third(0)
    e_third(1)
    for r in ORDER:
        parts = []
        for d in range(4):
            if (r, d) != (0, 0):
                ez[r, d].wait_recv()
                parts.append(zrecv[r, d].astype(F32))
            else:
                parts.append(zsend[0, zh].astype(F32))
        whole = sum(parts)
        slot = tok_of(r)
        ysend[slot, :, 0:128] = whole[:, 0:128]
        tail = whole[:, 128:256]
        ysend[slot, :, 128:256] = swap_halves(tail) if r % 2 else tail
    ey = [
        send(ysend.at[(y + d + 1) % 4], yrecv.at[d], ey_s.at[d], ey_r.at[d], at_y(d + 1)) for d in range(3)
    ]
    for copy in ey:
        copy.start()
    for copy in ey:
        copy.wait_recv()
    hid_ref[...] = (ysend[y] + yrecv[0] + yrecv[1] + yrecv[2]).astype(BF16)

    for copy in y_copies + list(z_copies.values()) + c_copies + list(ez.values()) + ey:
        copy.wait_send()
    for copies in list(x_first.values()) + list(x_second.values()):
        for copy in copies:
            copy.wait_send()
    for copy in list(e1.values()) + list(e2.values()):
        copy.wait_send()

    @pl.loop(0, 4)
    def _(j):
        to_sibling(j, out3, in3, b3_s, b3_r).wait_send()
        to_sibling(j, out1, in1, b1_s, b1_r).wait_send()
        cross_l(j).wait_send()
        cross_t(j).wait_send()
        d_sibling(j).wait_send()
        d_across(j).wait_send()
        d_relay(j).wait_send()


def body(hidden, hidden_tangent, head, head_tangent, ref_logits, actions, valid):
    h, g = hidden.T, hidden_tangent.T
    stacked = jnp.concatenate([h[:, 0:128], g[:, 0:128], h[:, 128:192], g[:, 128:192]], axis=1)
    acts = jnp.concatenate([actions, actions[128:]])[None, :]
    flags = jnp.concatenate([valid, valid[128:]])[None, :]
    vm, dma = pltpu.VMEM, pltpu.SemaphoreType.DMA
    vmem = pl.BlockSpec(memory_space=pltpu.VMEM)
    head_product, hid, tok = pl.pallas_call(
        kernel,
        out_shape=(
            jax.ShapeDtypeStruct((768, 1024), BF16),
            jax.ShapeDtypeStruct((48, 256), BF16),
            jax.ShapeDtypeStruct((2, 256), F32),
        ),
        in_specs=[vmem] * 6,
        out_specs=(vmem,) * 3,
        scratch_shapes=[
            vm((4, 256, 768), BF16),
            vm((4, 256, 768), BF16),
            vm((4, 384, 128), F32),
            vm((4, 48, 384), BF16),
            vm((4, 4, 4, 48, 384), BF16),
            vm((768, 1024), BF16),
            vm((768, 256), BF16),
            vm((4, 2, 384, 128), F32),
            vm((4, 2, 384, 128), F32),
            vm((4, 2, 384, 128), F32),
            vm((4, 2, 384, 128), F32),
            vm((4, 384, 128), F32),
            vm((4, 384, 128), BF16),
            vm((4, 384, 128), F32),
            vm((4, 384, 128), BF16),
            vm((4, 384, 128), F32),
            vm((4, 384, 128), F32),
            vm((3, 8, 256), F32),
            vm((3, 3, 8, 256), F32),
            vm((4, 4, 384, 128), BF16),
            vm((1024, 1024), BF16),
            vm((2, 4, 4, 48, 384), F32),
            vm((2, 2, 2, 48, 384), BF16),
            vm((2, 2, 2, 48, 384), BF16),
            vm((2, 2, 4, 48, 384), BF16),
            vm((2, 2, 4, 48, 384), BF16),
            vm((4, 4, 48, 256), BF16),
            vm((4, 4, 48, 256), BF16),
            vm((4, 48, 256), F32),
            vm((3, 48, 256), F32),
            dma((3,)), dma((3,)),
            dma((16,)), dma((16,)),
            dma((4, 4)), dma((4, 4)),
            dma((4,)), dma((4,)), dma((4,)), dma((4,)),
            dma((4,)), dma((4,)), dma((4,)), dma((4,)),
            dma((3, 3)), dma((3, 3)),
            dma((4,)), dma((4,)), dma((4,)), dma((4,)), dma((4,)), dma((4,)),
            dma((2, 2)), dma((2, 2)), dma((2, 2)), dma((2, 2)),
            dma((16,)), dma((16,)),
            dma((3,)), dma((3,)),
        ],
        compiler_params=pltpu.CompilerParams(
            collective_id=0, has_side_effects=True, vmem_limit_bytes=56 * 1024 * 1024
        ),
    )(stacked, head, head_tangent, ref_logits, acts, flags)
    return (head_product, hid[:, 0:192].T, tok[0, 0:192], tok[1, 0:192])


def solution(mesh):
    return jax.shard_map(
        body,
        mesh=mesh,
        in_specs=(P("tok", "vocab"),) * 5 + (P("tok"), P("tok")),
        out_specs=(P("tok", "vocab"), P("tok", "vocab"), P("tok"), P("tok")),
        check_vma=False,
    )
```

```python
import functools

import jax
import jax.numpy as jnp
from jax import lax
from jax.experimental import pallas as pl
from jax.experimental.pallas import tpu as pltpu
from jax.sharding import PartitionSpec as P

F32 = jnp.float32
BF16 = jnp.bfloat16
MESH = pl.DeviceIdType.MESH
ORDER = (3, 2, 1, 0)


def low_lanes(rows):
    return lax.broadcasted_iota(jnp.int32, (rows, 128), 1) < 64


def swap_halves(value):
    return pltpu.roll(value, 64, 1)


def merge(stats):
    tops = [s[0:1] for s in stats]
    ref_tops = [s[3:4] for s in stats]
    top = functools.reduce(jnp.maximum, tops)
    ref_top = functools.reduce(jnp.maximum, ref_tops)
    scale = [jnp.exp(a - top) for a in tops]
    ref_scale = [jnp.exp(a - ref_top) for a in ref_tops]
    n = range(len(stats))
    return (
        top,
        sum(stats[i][1:2] * scale[i] for i in n),
        sum(stats[i][2:3] * scale[i] for i in n),
        ref_top,
        sum(stats[i][4:5] * ref_scale[i] for i in n),
        sum(stats[i][5:6] * ref_scale[i] for i in n),
        sum(stats[i][6:7] for i in n),
    )


class Sent:
    def __init__(self, book, copy):
        self.book, self.copy, self.got = book, copy, False

    def start(self):
        self.copy.start()
        self.book.append(self)

    def wait_recv(self):
        self.copy.wait_recv()
        self.got = True

    def wait_send(self):
        self.copy.wait_send()


def kernel(
    h_ref, g_ref, head_hbm, ht_hbm, ref_hbm, act_ref, val_ref,
    hp_hbm, hid_ref, pen_ref, alp_ref,
    head_ref, ht_ref, ref_ref, hp_ref,
    head_t, ht_t, ref_t, sbk, hbuf, hun, tun,
    out3, in3, out1, in1, xl, xt, rl, rt, lg, tg,
    sst, sbuf, fbuf, fun, ep,
    e1s, e1r, e2s, e2r, zsend, zrecv, ysend, yrecv, ysum,
    in_sem, out_sem,
    ya_s, ya_r, za_s, za_r, xa_s, xa_r, b3_s, b3_r, b1_s, b1_r, bl_s, bl_r, bt_s, bt_r,
    c_s, c_r, d1_s, d1_r, d2_s, d2_r, d3_s, d3_r, e1_s, e1_q, e2_s, e2_q, ez_s, ez_r, ey_s, ey_r,
):
    loads = [
        pltpu.make_async_copy(src, dst, in_sem.at[i])
        for i, (src, dst) in enumerate(((head_hbm, head_ref), (ht_hbm, ht_ref), (ref_hbm, ref_ref)))
    ]
    for load in loads:
        load.start()
    v = lax.axis_index("vocab")
    t = lax.axis_index("tok")
    y, zh, x = v // 16, (v // 4) % 4, v % 4
    zl, c = t // 2, t % 2

    def at_x(d):
        return (v - x + (x + d) % 4, t)

    def at_xy(dx, dy):
        return ((y + dy) % 4 * 16 + zh * 4 + (x + dx) % 4, t)

    def at_y(d):
        return ((y + d) % 4 * 16 + zh * 4 + x, t)

    def tok_of(r):
        return (zl + r // 2) % 2 * 2 + (c + r % 2) % 2

    def at_z(r, d):
        return (y * 16 + (zh + d) % 4 * 4 + x, tok_of(r))

    sent, loops = [], []

    def send(src, dst, ssem, rsem, device):
        return Sent(
            sent,
            pltpu.make_async_remote_copy(
                src_ref=src, dst_ref=dst, send_sem=ssem, recv_sem=rsem,
                device_id=device, device_id_type=MESH,
            ),
        )

    def raw(src, dst, ssem, rsem, device):
        return send(src, dst, ssem, rsem, device).copy

    def finish():
        zy_finish()
        for copy in sent:
            copy.wait_send()
        if loops:

            @pl.loop(0, 4)
            def _(j):
                for copy_of in loops:
                    copy_of(j).wait_send()

    barrier = pltpu.get_barrier_semaphore()
    column = [(r, d) for r in ORDER for d in range(4) if (r, d) != (0, 0)]
    plane = [(dx, dy) for dx in range(4) for dy in range(4) if (dx, dy) != (0, 0)]
    peers = [at_xy(dx, dy) for dx, dy in plane] + [at_z(r, d) for r, d in column]
    for peer in peers:
        pl.semaphore_signal(barrier, inc=1, device_id=peer, device_id_type=MESH)
    pl.semaphore_wait(barrier, len(peers))

    h, g = h_ref[...].astype(F32), g_ref[...].astype(F32)
    sbk[:, 0:128] = h[:, 0:128].astype(BF16)
    sbk[:, 128:256] = g[:, 0:128].astype(BF16)
    sbk[:, 256:384] = jnp.concatenate([h[:, 128:192], g[:, 128:192]], axis=1).astype(BF16)
    slot = (zl + y // 2) % 2 * 2 + (c + y % 2) % 2

    def z_copy(d):
        device = (y * 16 + (zh + d) % 4 * 4 + x, y)
        return raw(sbk, hbuf.at[slot, zh, x], za_s.at[d], za_r.at[slot * 4 + d], device)

    def z_wait(r, d):
        into = hbuf.at[r, (zh + 4 - d) % 4, x]
        raw(sbk, into, za_s.at[d], za_r.at[r * 4 + d], at_z(r, 1)).wait_recv()

    for d in (1, 2, 3):
        z_copy(d).start()

    @pl.when(t != y)
    def _():
        z_copy(0).start()

    @pl.when(t == y)
    def _():
        hbuf[0, zh, x] = sbk[...]

    away = (y + 4 - t) % 4

    def y_copy(r, k):
        part = hbuf.at[r, :, x] if k < 2 else hbuf.at[r, (k - 2) * 2 : (k - 2) * 2 + 2, x]
        return raw(part, part, ya_s.at[r, k], ya_r.at[r, k], at_y(3 if k % 2 else 1))

    def y_stage(r):
        @pl.when(away == 0)
        def _():
            for d in range(4):
                if (r, d) != (0, 0):
                    z_wait(r, d)
            y_copy(r, 0).start()
            y_copy(r, 1).start()

        @pl.when(away == 1)
        def _():
            y_copy(r, 0).wait_recv()
            y_copy(r, 2).start()

        @pl.when(away == 3)
        def _():
            y_copy(r, 1).wait_recv()
            y_copy(r, 3).start()

        @pl.when(away == 2)
        def _():
            y_copy(r, 2).wait_recv()
            y_copy(r, 3).wait_recv()

    def zy_finish():
        for d in (1, 2, 3):
            z_copy(d).wait_send()

        @pl.when(t != y)
        def _():
            z_copy(0).wait_send()

        for role, kinds in ((0, (0, 1)), (1, (2,)), (3, (3,))):

            @pl.when(away == role)
            def _():
                for r in range(4):
                    for k in kinds:
                        y_copy(r, k).wait_send()

    for load in loads:
        load.wait()
    for j in range(4):
        for half in range(2):
            cols = slice(half * 512 + j * 128, half * 512 + j * 128 + 128)
            head_t[j, half * 128 : half * 128 + 128] = head_ref[:, cols].T
            ht_t[j, half * 128 : half * 128 + 128] = ht_ref[:, cols].T
            ref_t[j, half * 128 : half * 128 + 128] = ref_ref[0:128, cols].astype(F32).T
        a, b = slice(j * 128, j * 128 + 128), slice(512 + j * 128, 512 + j * 128 + 128)
        tails = jnp.concatenate([ref_ref[128:192, a].astype(F32), ref_ref[128:192, b].astype(F32)], axis=0)
        ref_t[j, 256:384] = tails.T

    left_x, right_x = (x + 3) % 4, (x + 1) % 4
    x_first, x_second = {}, {}
    for r in ORDER:
        own = hbuf.at[r, :, x]
        x_first[r] = (
            send(own, own, xa_s.at[r, 0], xa_r.at[r, 0], at_x(1)),
            send(own, own, xa_s.at[r, 1], xa_r.at[r, 1], at_x(3)),
        )
        from_left = hbuf.at[r, 0:2, left_x]
        from_right = hbuf.at[r, 2:4, right_x]
        x_second[r] = (
            send(from_left, from_left, xa_s.at[r, 2], xa_r.at[r, 2], at_x(1)),
            send(from_right, from_right, xa_s.at[r, 3], xa_r.at[r, 3], at_x(3)),
        )

    def x_start(r):
        y_stage(r)
        for copy in x_first[r]:
            copy.start()

    def x_forward(r):
        for first, second in zip(x_first[r], x_second[r]):
            first.wait_recv()
            second.start()

    def unpack(r):
        for copy in x_second[r]:
            copy.wait_recv()
        low = low_lanes(768)
        block = hbuf[r].reshape(768, 384)
        tails = block[:, 256:384].astype(F32)
        other = swap_halves(tails)
        hun[:, r * 256 : r * 256 + 128] = block[:, 0:128]
        hun[:, r * 256 + 128 : r * 256 + 256] = jnp.where(low, tails, other).astype(BF16)
        tun[:, 0:128] = block[:, 128:256]
        tun[:, 128:256] = jnp.where(low, other, tails).astype(BF16)

    low128 = low_lanes(128)

    def pack(value):
        tail = jnp.where(low128, value[0:128, 128:256], value[128:256, 128:256])
        return value[:, 0:128], tail

    def partial(r, j):
        h = hun[:, r * 256 : r * 256 + 256]
        logits = jnp.dot(head_t[j], h, preferred_element_type=F32)
        tangent = jnp.dot(head_t[j], tun[...], preferred_element_type=F32) + jnp.dot(
            ht_t[j], h, preferred_element_type=F32
        )
        return pack(logits) + pack(tangent)

    sibling = (v, tok_of(1))
    across = (v, tok_of(2))

    def to_sibling(j, out, into, ssem, rsem):
        return raw(out.at[j], into.at[j], ssem.at[j], rsem.at[j], sibling)

    def cross_l(j):
        return raw(xl.at[j], rl.at[j], bl_s.at[j], bl_r.at[j], across)

    def cross_t(j):
        return raw(xt.at[j], rt.at[j], bt_s.at[j], bt_r.at[j], across)

    def give(r, out, into, ssem, rsem):
        @pl.loop(0, 4)
        def _(j):
            lm, lt, tm, tt = partial(r, j)
            out[j, 0, 0:256] = lm
            out[j, 0, 256:384] = lt
            out[j, 1, 0:256] = tm
            out[j, 1, 256:384] = tt
            to_sibling(j, out, into, ssem, rsem).start()

    x_start(3)
    x_start(2)
    x_forward(3)
    x_forward(2)
    unpack(3)
    give(3, out3, in3, b3_s, b3_r)
    loops.append(lambda j: to_sibling(j, out3, in3, b3_s, b3_r))
    unpack(2)

    @pl.loop(0, 4)
    def _(j):
        lm, lt, tm, tt = partial(2, j)
        to_sibling(j, out3, in3, b3_s, b3_r).wait_recv()
        xl[j, 0:256] = lm + in3[j, 0, 0:256]
        xl[j, 256:384] = lt + in3[j, 0, 256:384]
        xt[j, 0:256] = (tm + in3[j, 1, 0:256]).astype(BF16)
        xt[j, 256:384] = (tt + in3[j, 1, 256:384]).astype(BF16)
        cross_l(j).start()
        cross_t(j).start()

    loops += [cross_l, cross_t]
    x_start(1)
    x_start(0)
    x_forward(1)
    x_forward(0)
    unpack(1)
    give(1, out1, in1, b1_s, b1_r)
    loops.append(lambda j: to_sibling(j, out1, in1, b1_s, b1_r))
    unpack(0)

    @pl.loop(0, 4)
    def _(j):
        lm, lt, tm, tt = partial(0, j)
        to_sibling(j, out1, in1, b1_s, b1_r).wait_recv()
        lg[j, 0:256] = lm + in1[j, 0, 0:256]
        lg[j, 256:384] = lt + in1[j, 0, 256:384]
        tg[j, 0:256] = tm + in1[j, 1, 0:256]
        tg[j, 256:384] = tt + in1[j, 1, 256:384]

    lowest = jnp.full((1, 128), -jnp.inf, F32)

    def maxima(j, carry):
        top_m, top_t, ref_m, ref_tl = carry
        cross_l(j).wait_recv()
        cross_t(j).wait_recv()
        logits = lg[j] + rl[j]
        lg[j] = logits
        tg[j] = tg[j] + rt[j].astype(F32)
        ref = ref_t[j]
        return (
            jnp.maximum(top_m, jnp.max(logits[0:256], 0, keepdims=True)),
            jnp.maximum(top_t, jnp.max(logits[256:384], 0, keepdims=True)),
            jnp.maximum(ref_m, jnp.max(ref[0:256], 0, keepdims=True)),
            jnp.maximum(ref_tl, jnp.max(ref[256:384], 0, keepdims=True)),
        )

    top_m, top_t, ref_m, ref_tl = lax.fori_loop(0, 4, maxima, (lowest,) * 4)
    top_t = jnp.maximum(top_t, swap_halves(top_t))
    ref_tl = jnp.maximum(ref_tl, swap_halves(ref_tl))

    row = lax.broadcasted_iota(jnp.int32, (256, 128), 0)
    main_col = jnp.where(row < 128, row, row + 384)
    tail_row = lax.broadcasted_iota(jnp.int32, (128, 128), 0)
    tail_col = jnp.where(low128, tail_row, tail_row + 512)
    wanted = act_ref[...] - v * 1024
    wanted_m = wanted[:, 0:128]
    wanted_t = jnp.concatenate([wanted[:, 128:192]] * 2, axis=1)

    def sums(j, carry):
        def part(logits, tangent, ref, top, ref_top, col, wanted, old):
            weights = jnp.exp(logits - top)
            ref_weights = jnp.exp(ref - ref_top)
            picked = jnp.where(col + j * 128 == wanted, logits, 0.0)
            new = (weights, weights * tangent, ref_weights, ref_weights * (ref - logits), picked)
            return tuple(o + jnp.sum(n, 0, keepdims=True) for o, n in zip(old, new))

        main = part(lg[j, 0:256], tg[j, 0:256], ref_t[j, 0:256], top_m, ref_m, main_col, wanted_m, carry[0:5])
        tail = part(
            lg[j, 256:384], tg[j, 256:384], ref_t[j, 256:384], top_t, ref_tl, tail_col, wanted_t, carry[5:10]
        )
        return main + tail

    found = lax.fori_loop(0, 4, sums, (jnp.zeros((1, 128), F32),) * 10)
    tails = [value + swap_halves(value) for value in found[5:10]]
    rows_m = [top_m, found[0], found[1], ref_m, found[2], found[3], found[4]]
    rows_t = [top_t, tails[0], tails[1], ref_tl, tails[2], tails[3], tails[4]]
    for i in range(7):
        sst[0, i : i + 1, 0:128] = rows_m[i]
        sst[0, i : i + 1, 128:256] = rows_t[i]
    sst[:, 7:8] = jnp.zeros((2, 1, 256), F32)

    now = [send(sst.at[0], sbuf.at[i], c_s.at[i], c_r.at[i], at_xy(*plane[i])) for i in range(15)]
    for copy in now:
        copy.start()
    for copy in now:
        copy.wait_recv()
    merged = merge([sst[0]] + [sbuf[i] for i in range(15)])
    for i in range(7):
        sst[1, i : i + 1] = merged[i]
    now = [send(sst.at[1], sbuf.at[i], c_s.at[i], c_r.at[i], at_z(0, i - 14)) for i in range(15, 18)]
    for copy in now:
        copy.start()
    for copy in now:
        copy.wait_recv()
    merged = merge([sst[1]] + [sbuf[i] for i in range(15, 18)])

    top, total, moment, ref_top, ref_sum, cross, chosen = merged
    log_total = top + jnp.log(total)
    mean_tangent = moment / total
    valid = val_ref[...].astype(F32)
    valid = jnp.concatenate([valid, valid[:, 128:192]], axis=1)
    penalty = valid * (cross / ref_sum - (ref_top + jnp.log(ref_sum)) + log_total)
    pen_ref[...] = penalty[:, 0:192]
    alp_ref[...] = (chosen - log_total)[:, 0:192]

    def d_sibling(j):
        return raw(fbuf.at[0, j], fbuf.at[1, j], d1_s.at[j], d1_r.at[j], sibling)

    def d_across(j):
        return raw(fbuf.at[0, j], fbuf.at[2, j], d2_s.at[j], d2_r.at[j], across)

    def d_relay(j):
        return raw(fbuf.at[2, j], fbuf.at[3, j], d3_s.at[j], d3_r.at[j], sibling)

    @pl.loop(0, 4)
    def _(j):
        def part(rows, lanes):
            return (
                valid[:, lanes] * jnp.exp(lg[j, rows] - log_total[:, lanes]) * (tg[j, rows] - mean_tangent[:, lanes])
            ).astype(BF16)

        fbuf[0, j, 0:256] = part(slice(0, 256), slice(0, 128))
        fbuf[0, j, 256:384] = part(slice(256, 384), slice(128, 256))
        d_across(j).start()
        d_sibling(j).start()

    def unpack_fisher(r):
        for j in range(4):
            block = fbuf[r, j]
            tail = block[256:384]
            zero = jnp.zeros_like(tail)
            for half in range(2):
                rows = slice(half * 512 + j * 128, half * 512 + j * 128 + 128)
                fun[rows, r * 256 : r * 256 + 128] = block[half * 128 : half * 128 + 128]
                fun[rows, r * 256 + 128 : r * 256 + 256] = (
                    jnp.where(low128, tail, zero) if half == 0 else jnp.where(low128, zero, tail)
                )

    low192 = low_lanes(192)

    def hidden_part(p):
        @pl.loop(0, 4)
        def _(k):
            rows = pl.ds(pl.multiple_of(k * 192, 192), 192)
            part = jnp.dot(head_ref[rows, :], fun[:, p * 512 : p * 512 + 512], preferred_element_type=F32)
            even, odd = part[:, 128:256], part[:, 384:512]
            tail = jnp.where(low192, even + swap_halves(even), odd + swap_halves(odd))
            ep[p, k, :, :, 0:128] = part[:, 0:128].reshape(4, 48, 128)
            ep[p, k, :, :, 128:256] = part[:, 256:384].reshape(4, 48, 128)
            ep[p, k, :, :, 256:384] = tail.reshape(4, 48, 128)

    e1, e2 = {}, {}
    for p in range(2):
        for side, d in ((0, 1), (1, 3)):
            e1[p, side] = send(e1s.at[p, side], e1r.at[p, side], e1_s.at[p, side], e1_q.at[p, side], at_x(d))
            e2[p, side] = send(e2s.at[p, side], e2r.at[p, side], e2_s.at[p, side], e2_q.at[p, side], at_x(d))

    def e_first(p):
        far = (x + 2) % 4
        e1s[p, 0] = ep[p, 0:2, far].astype(BF16)
        e1s[p, 1] = ep[p, 2:4, far].astype(BF16)
        e1[p, 0].start()
        e1[p, 1].start()

    def e_second(p):
        e2s[p, 0, 2:4] = ep[p, 2:4, right_x].astype(BF16)
        e2s[p, 1, 0:2] = ep[p, 0:2, left_x].astype(BF16)
        e1[p, 0].wait_recv()
        e2s[p, 0, 0:2] = (ep[p, 0:2, right_x] + e1r[p, 0].astype(F32)).astype(BF16)
        e2[p, 0].start()
        e1[p, 1].wait_recv()
        e2s[p, 1, 2:4] = (ep[p, 2:4, left_x] + e1r[p, 1].astype(F32)).astype(BF16)
        e2[p, 1].start()

    ez = {
        (r, d): send(
            zsend.at[r, (zh + d) % 4], zrecv.at[r, d], ez_s.at[r * 4 + d], ez_r.at[r * 4 + d], at_z(r, d)
        )
        for r, d in column
    }

    def e_third(p):
        e2[p, 0].wait_recv()
        e2[p, 1].wait_recv()
        total_x = (ep[p, :, x] + e2r[p, 0].astype(F32) + e2r[p, 1].astype(F32)).astype(BF16)
        for odd in range(2):
            zsend[p * 2 + odd, :, :, 0:128] = total_x[:, :, odd * 128 : odd * 128 + 128]
            zsend[p * 2 + odd, :, :, 128:256] = total_x[:, :, 256:384]
        for r in (p * 2 + 1, p * 2):
            for d in range(4):
                if (r, d) != (0, 0):
                    ez[r, d].start()

    loops += [d_across, d_sibling]
    unpack_fisher(0)
    for j in range(4):
        d_sibling(j).wait_recv()
    unpack_fisher(1)
    for j in range(2):
        d_across(j).wait_recv()
        d_relay(j).start()
    hidden_part(0)
    e_first(0)
    for j in range(2, 4):
        d_across(j).wait_recv()
        d_relay(j).start()
    loops.append(d_relay)
    e_second(0)
    unpack_fisher(2)
    for j in range(4):
        d_relay(j).wait_recv()
    unpack_fisher(3)
    hidden_part(1)
    e_first(1)

    def product(k):
        rows = slice(k * 256, k * 256 + 256)
        return pltpu.make_async_copy(hp_ref.at[rows], hp_hbm.at[rows], out_sem.at[k])

    def head_part(k):
        rows = slice(k * 256, k * 256 + 256)

        @pl.loop(0, 2)
        def _(n):
            cols = pl.ds(pl.multiple_of(n * 512, 512), 512)
            hp_ref[rows, cols] = lax.dot_general(
                hun[rows, :], fun[cols, :], (((1,), (1,)), ((), ())), preferred_element_type=F32
            ).astype(BF16)

        product(k).start()

    e_third(0)
    head_part(0)
    e_second(1)
    head_part(1)
    e_third(1)
    head_part(2)
    for r in ORDER:
        parts = []
        for d in range(4):
            if (r, d) != (0, 0):
                ez[r, d].wait_recv()
                parts.append(zrecv[r, d].astype(F32))
            else:
                parts.append(zsend[0, zh].astype(F32))
        whole = sum(parts)
        place = tok_of(r)
        tail = swap_halves(whole[:, 128:256]) if r % 2 else whole[:, 128:256]
        ysum[place, :, 0:128] = whole[:, 0:128]
        ysum[place, :, 128:256] = tail
        ysend[place, :, 0:128] = whole[:, 0:128].astype(BF16)
        ysend[place, :, 128:256] = tail.astype(BF16)
    ey = [
        send(ysend.at[(y + d + 1) % 4], yrecv.at[d], ey_s.at[d], ey_r.at[d], at_y(d + 1)) for d in range(3)
    ]
    for copy in ey:
        copy.start()
    for copy in ey:
        copy.wait_recv()
    total_y = ysum[y] + sum(yrecv[d].astype(F32) for d in range(3))
    hid_ref[...] = total_y[:, 0:192].astype(BF16)
    finish()
    for k in range(3):
        product(k).wait()


def copy_out(*refs):
    big, in_sem, out_sem = refs[8:]
    copies = []
    for k in range(4):
        rows = slice(k * 192, k * 192 + 192)
        copies.append(
            (
                pltpu.make_async_copy(refs[0].at[rows], big.at[rows], in_sem.at[k]),
                pltpu.make_async_copy(big.at[rows], refs[4].at[rows], out_sem.at[k]),
            )
        )
    for load, _ in copies:
        load.start()
    for i in range(1, 4):
        refs[4 + i][...] = refs[i][...]
    for load, store in copies:
        load.wait()
        store.start()
    for _, store in copies:
        store.wait()


def body(hidden, hidden_tangent, head, head_tangent, ref_logits, actions, valid):
    vm, dma = pltpu.VMEM, pltpu.SemaphoreType.DMA
    vmem = pl.BlockSpec(memory_space=pltpu.VMEM)
    hbm = pl.BlockSpec(memory_space=pl.ANY)
    shapes = (
        jax.ShapeDtypeStruct((768, 1024), BF16),
        jax.ShapeDtypeStruct((48, 192), BF16),
        jax.ShapeDtypeStruct((1, 192), F32),
        jax.ShapeDtypeStruct((1, 192), F32),
    )
    results = pl.pallas_call(
        kernel,
        out_shape=shapes,
        in_specs=[vmem, vmem, hbm, hbm, hbm, vmem, vmem],
        out_specs=(hbm, vmem, vmem, vmem),
        scratch_shapes=[
            vm((768, 1024), BF16),
            vm((768, 1024), BF16),
            vm((192, 1024), BF16),
            vm((768, 1024), BF16),
            vm((4, 256, 768), BF16),
            vm((4, 256, 768), BF16),
            vm((4, 384, 128), F32),
            vm((48, 384), BF16),
            vm((4, 4, 4, 48, 384), BF16),
            vm((768, 1024), BF16),
            vm((768, 256), BF16),
            vm((4, 2, 384, 128), F32),
            vm((4, 2, 384, 128), F32),
            vm((4, 2, 384, 128), F32),
            vm((4, 2, 384, 128), F32),
            vm((4, 384, 128), F32),
            vm((4, 384, 128), BF16),
            vm((4, 384, 128), F32),
            vm((4, 384, 128), BF16),
            vm((4, 384, 128), F32),
            vm((4, 384, 128), F32),
            vm((2, 8, 256), F32),
            vm((18, 8, 256), F32),
            vm((4, 4, 384, 128), BF16),
            vm((1024, 1024), BF16),
            vm((2, 4, 4, 48, 384), F32),
            vm((2, 2, 2, 48, 384), BF16),
            vm((2, 2, 2, 48, 384), BF16),
            vm((2, 2, 4, 48, 384), BF16),
            vm((2, 2, 4, 48, 384), BF16),
            vm((4, 4, 48, 256), BF16),
            vm((4, 4, 48, 256), BF16),
            vm((4, 48, 256), BF16),
            vm((3, 48, 256), BF16),
            vm((4, 48, 256), F32),
            dma((3,)), dma((3,)),
            dma((4, 4)), dma((4, 4)),
            dma((4,)), dma((16,)),
            dma((4, 4)), dma((4, 4)),
            dma((4,)), dma((4,)), dma((4,)), dma((4,)),
            dma((4,)), dma((4,)), dma((4,)), dma((4,)),
            dma((18,)), dma((18,)),
            dma((4,)), dma((4,)), dma((4,)), dma((4,)), dma((4,)), dma((4,)),
            dma((2, 2)), dma((2, 2)), dma((2, 2)), dma((2, 2)),
            dma((16,)), dma((16,)),
            dma((3,)), dma((3,)),
        ],
        compiler_params=pltpu.CompilerParams(
            collective_id=0, has_side_effects=True, vmem_limit_bytes=56 * 1024 * 1024
        ),
    )(hidden.T, hidden_tangent.T, head, head_tangent, ref_logits, actions[None, :], valid[None, :])
    head_product, hid, penalty, logprob = pl.pallas_call(
        copy_out,
        out_shape=shapes,
        in_specs=[hbm, vmem, vmem, vmem],
        out_specs=(hbm, vmem, vmem, vmem),
        scratch_shapes=[vm((768, 1024), BF16), dma((4,)), dma((4,))],
    )(*results)
    return (head_product, hid.T, penalty.reshape(192), logprob.reshape(192))


def solution(mesh):
    return jax.shard_map(
        body,
        mesh=mesh,
        in_specs=(P("tok", "vocab"),) * 5 + (P("tok"), P("tok")),
        out_specs=(P("tok", "vocab"), P("tok", "vocab"), P("tok"), P("tok")),
        check_vma=False,
    )
```

```python
import functools

import jax
import jax.numpy as jnp
from jax import lax
from jax.experimental import pallas as pl
from jax.experimental.pallas import tpu as pltpu
from jax.sharding import PartitionSpec as P

F32 = jnp.float32
BF16 = jnp.bfloat16
MESH = pl.DeviceIdType.MESH
ORDER = (3, 2, 1, 0)


def low_lanes(rows):
    return lax.broadcasted_iota(jnp.int32, (rows, 128), 1) < 64


def swap_halves(value):
    return pltpu.roll(value, 64, 1)


def merge(stats):
    tops = [s[0:1] for s in stats]
    ref_tops = [s[3:4] for s in stats]
    top = functools.reduce(jnp.maximum, tops)
    ref_top = functools.reduce(jnp.maximum, ref_tops)
    scale = [jnp.exp(a - top) for a in tops]
    ref_scale = [jnp.exp(a - ref_top) for a in ref_tops]
    n = range(len(stats))
    return (
        top,
        sum(stats[i][1:2] * scale[i] for i in n),
        sum(stats[i][2:3] * scale[i] for i in n),
        ref_top,
        sum(stats[i][4:5] * ref_scale[i] for i in n),
        sum(stats[i][5:6] * ref_scale[i] for i in n),
        sum(stats[i][6:7] for i in n),
    )


class Sent:
    def __init__(self, book, copy):
        self.book, self.copy, self.got = book, copy, False

    def start(self):
        self.copy.start()
        self.book.append(self)

    def wait_recv(self):
        self.copy.wait_recv()
        self.got = True

    def wait_send(self):
        self.copy.wait_send()


def kernel(
    h_hbm, g_hbm, head_hbm, ht_hbm, ref_hbm, act_hbm, val_hbm,
    hp_hbm, hid_hbm, pen_hbm, alp_hbm,
    h_ref, g_ref, act_ref, val_ref, hid_ref, pen_ref, alp_ref,
    head_ref, ht_ref, ref_ref, hp_ref,
    head_t, ht_t, ref_t, sbk, hbuf, hun, tun,
    out3, in3, out1, in1, xl, xt, rl, rt, lg, tg,
    sst, sbuf, fbuf, fun, ep,
    e1s, e1r, e2s, e2r, zsend, zrecv, ysend, yrecv, ysum,
    in_sem, out_sem,
    ya_s, ya_r, za_s, za_r, xa_s, xa_r, b3_s, b3_r, b1_s, b1_r, bl_s, bl_r, bt_s, bt_r,
    c_s, c_r, d1_s, d1_r, d2_s, d2_r, d3_s, d3_r, e1_s, e1_q, e2_s, e2_q, ez_s, ez_r, ey_s, ey_r,
):
    loads = [
        pltpu.make_async_copy(src, dst, in_sem.at[i])
        for i, (src, dst) in enumerate(
            (
                (h_hbm, h_ref), (g_hbm, g_ref), (head_hbm, head_ref), (ht_hbm, ht_ref),
                (ref_hbm, ref_ref), (act_hbm, act_ref), (val_hbm, val_ref),
            )
        )
    ]
    for load in loads:
        load.start()
    v = lax.axis_index("vocab")
    t = lax.axis_index("tok")
    y, zh, x = v // 16, (v // 4) % 4, v % 4
    zl, c = t // 2, t % 2

    def at_x(d):
        return (v - x + (x + d) % 4, t)

    def at_xy(dx, dy):
        return ((y + dy) % 4 * 16 + zh * 4 + (x + dx) % 4, t)

    def at_y(d):
        return ((y + d) % 4 * 16 + zh * 4 + x, t)

    def tok_of(r):
        return (zl + r // 2) % 2 * 2 + (c + r % 2) % 2

    def at_z(r, d):
        return (y * 16 + (zh + d) % 4 * 4 + x, tok_of(r))

    sent, loops = [], []

    def send(src, dst, ssem, rsem, device):
        return Sent(
            sent,
            pltpu.make_async_remote_copy(
                src_ref=src, dst_ref=dst, send_sem=ssem, recv_sem=rsem,
                device_id=device, device_id_type=MESH,
            ),
        )

    def raw(src, dst, ssem, rsem, device):
        return send(src, dst, ssem, rsem, device).copy

    def finish():
        zy_finish()
        for copy in sent:
            copy.wait_send()
        if loops:

            @pl.loop(0, 4)
            def _(j):
                for copy_of in loops:
                    copy_of(j).wait_send()

    barrier = pltpu.get_barrier_semaphore()
    column = [(r, d) for r in ORDER for d in range(4) if (r, d) != (0, 0)]
    plane = [(dx, dy) for dx in range(4) for dy in range(4) if (dx, dy) != (0, 0)]
    peers = [at_xy(dx, dy) for dx, dy in plane] + [at_z(r, d) for r, d in column]
    for peer in peers:
        pl.semaphore_signal(barrier, inc=1, device_id=peer, device_id_type=MESH)
    for load in loads:
        load.wait()
    h, g = h_ref[...].astype(F32), g_ref[...].astype(F32)
    sbk[:, 0:128] = h[:, 0:128].astype(BF16)
    sbk[:, 128:256] = g[:, 0:128].astype(BF16)
    sbk[:, 256:384] = jnp.concatenate([h[:, 128:192], g[:, 128:192]], axis=1).astype(BF16)

    def turn(src, dst, j):
        for half in range(2):
            cols = slice(half * 512 + j * 128, half * 512 + j * 128 + 128)
            dst[j, half * 128 : half * 128 + 128] = src[:, cols].T

    def turn_ref(j):
        a, b = slice(j * 128, j * 128 + 128), slice(512 + j * 128, 512 + j * 128 + 128)
        ref_t[j, 0:128] = ref_ref[0:128, a].astype(F32).T
        ref_t[j, 128:256] = ref_ref[0:128, b].astype(F32).T
        tails = jnp.concatenate([ref_ref[128:192, a].astype(F32), ref_ref[128:192, b].astype(F32)], axis=0)
        ref_t[j, 256:384] = tails.T

    turn(head_ref, head_t, 0)
    turn(head_ref, head_t, 1)
    turn(head_ref, head_t, 2)

    pl.semaphore_wait(barrier, len(peers))

    slot = (zl + y // 2) % 2 * 2 + (c + y % 2) % 2

    def z_copy(d):
        device = (y * 16 + (zh + d) % 4 * 4 + x, y)
        return raw(sbk, hbuf.at[slot, zh, x], za_s.at[d], za_r.at[slot * 4 + d], device)

    def z_wait(r, d):
        into = hbuf.at[r, (zh + 4 - d) % 4, x]
        raw(sbk, into, za_s.at[d], za_r.at[r * 4 + d], at_z(r, 1)).wait_recv()

    for d in (1, 2, 3):
        z_copy(d).start()

    @pl.when(t != y)
    def _():
        z_copy(0).start()

    @pl.when(t == y)
    def _():
        hbuf[0, zh, x] = sbk[...]

    away = (y + 4 - t) % 4

    def y_copy(r, k):
        part = hbuf.at[r, :, x] if k < 2 else hbuf.at[r, (k - 2) * 2 : (k - 2) * 2 + 2, x]
        return raw(part, part, ya_s.at[r, k], ya_r.at[r, k], at_y(3 if k % 2 else 1))

    def y_stage(r):
        @pl.when(away == 0)
        def _():
            for d in range(4):
                if (r, d) != (0, 0):
                    z_wait(r, d)
            y_copy(r, 0).start()
            y_copy(r, 1).start()

        @pl.when(away == 1)
        def _():
            y_copy(r, 0).wait_recv()
            y_copy(r, 2).start()

        @pl.when(away == 3)
        def _():
            y_copy(r, 1).wait_recv()
            y_copy(r, 3).start()

        @pl.when(away == 2)
        def _():
            y_copy(r, 2).wait_recv()
            y_copy(r, 3).wait_recv()

    def zy_finish():
        for d in (1, 2, 3):
            z_copy(d).wait_send()

        @pl.when(t != y)
        def _():
            z_copy(0).wait_send()

        for role, kinds in ((0, (0, 1)), (1, (2,)), (3, (3,))):

            @pl.when(away == role)
            def _():
                for r in range(4):
                    for k in kinds:
                        y_copy(r, k).wait_send()

    left_x, right_x = (x + 3) % 4, (x + 1) % 4
    x_first, x_second = {}, {}
    for r in ORDER:
        own = hbuf.at[r, :, x]
        x_first[r] = (
            send(own, own, xa_s.at[r, 0], xa_r.at[r, 0], at_x(1)),
            send(own, own, xa_s.at[r, 1], xa_r.at[r, 1], at_x(3)),
        )
        from_left = hbuf.at[r, 0:2, left_x]
        from_right = hbuf.at[r, 2:4, right_x]
        x_second[r] = (
            send(from_left, from_left, xa_s.at[r, 2], xa_r.at[r, 2], at_x(1)),
            send(from_right, from_right, xa_s.at[r, 3], xa_r.at[r, 3], at_x(3)),
        )

    def x_start(r):
        y_stage(r)
        for copy in x_first[r]:
            copy.start()

    def x_forward(r):
        for first, second in zip(x_first[r], x_second[r]):
            first.wait_recv()
            second.start()

    def unpack(r):
        for copy in x_second[r]:
            copy.wait_recv()
        low = low_lanes(768)
        block = hbuf[r].reshape(768, 384)
        tails = block[:, 256:384].astype(F32)
        other = swap_halves(tails)
        hun[:, r * 256 : r * 256 + 128] = block[:, 0:128]
        hun[:, r * 256 + 128 : r * 256 + 256] = jnp.where(low, tails, other).astype(BF16)
        tun[:, 0:128] = block[:, 128:256]
        tun[:, 128:256] = jnp.where(low, other, tails).astype(BF16)

    low128 = low_lanes(128)

    def pack(value):
        tail = jnp.where(low128, value[0:128, 128:256], value[128:256, 128:256])
        return value[:, 0:128], tail

    def partial(r, j):
        h = hun[:, r * 256 : r * 256 + 256]
        logits = jnp.dot(head_t[j], h, preferred_element_type=F32)
        tangent = jnp.dot(head_t[j], tun[...], preferred_element_type=F32) + jnp.dot(
            ht_t[j], h, preferred_element_type=F32
        )
        return pack(logits) + pack(tangent)

    sibling = (v, tok_of(1))
    across = (v, tok_of(2))

    def to_sibling(j, out, into, ssem, rsem):
        return raw(out.at[j], into.at[j], ssem.at[j], rsem.at[j], sibling)

    def cross_l(j):
        return raw(xl.at[j], rl.at[j], bl_s.at[j], bl_r.at[j], across)

    def cross_t(j):
        return raw(xt.at[j], rt.at[j], bt_s.at[j], bt_r.at[j], across)

    def give(r, out, into, ssem, rsem):
        @pl.loop(0, 4)
        def _(j):
            lm, lt, tm, tt = partial(r, j)
            out[j, 0, 0:256] = lm
            out[j, 0, 256:384] = lt
            out[j, 1, 0:256] = tm
            out[j, 1, 256:384] = tt
            to_sibling(j, out, into, ssem, rsem).start()

    turn(head_ref, head_t, 3)
    x_start(3)
    turn(ht_ref, ht_t, 0)
    x_start(2)
    turn(ht_ref, ht_t, 1)
    x_forward(3)
    turn(ht_ref, ht_t, 2)
    x_forward(2)
    turn(ht_ref, ht_t, 3)
    unpack(3)
    give(3, out3, in3, b3_s, b3_r)
    loops.append(lambda j: to_sibling(j, out3, in3, b3_s, b3_r))
    unpack(2)

    @pl.loop(0, 4)
    def _(j):
        lm, lt, tm, tt = partial(2, j)
        to_sibling(j, out3, in3, b3_s, b3_r).wait_recv()
        xl[j, 0:256] = lm + in3[j, 0, 0:256]
        xl[j, 256:384] = lt + in3[j, 0, 256:384]
        xt[j, 0:256] = (tm + in3[j, 1, 0:256]).astype(BF16)
        xt[j, 256:384] = (tt + in3[j, 1, 256:384]).astype(BF16)
        cross_l(j).start()
        cross_t(j).start()

    loops += [cross_l, cross_t]
    x_start(1)
    x_start(0)
    x_forward(1)
    for j in range(4):
        turn_ref(j)
    x_forward(0)
    unpack(1)
    give(1, out1, in1, b1_s, b1_r)
    loops.append(lambda j: to_sibling(j, out1, in1, b1_s, b1_r))
    unpack(0)

    @pl.loop(0, 4)
    def _(j):
        lm, lt, tm, tt = partial(0, j)
        to_sibling(j, out1, in1, b1_s, b1_r).wait_recv()
        lg[j, 0:256] = lm + in1[j, 0, 0:256]
        lg[j, 256:384] = lt + in1[j, 0, 256:384]
        tg[j, 0:256] = tm + in1[j, 1, 0:256]
        tg[j, 256:384] = tt + in1[j, 1, 256:384]

    lowest = jnp.full((1, 128), -jnp.inf, F32)

    def maxima(j, carry):
        top_m, top_t, ref_m, ref_tl = carry
        cross_l(j).wait_recv()
        cross_t(j).wait_recv()
        logits = lg[j] + rl[j]
        lg[j] = logits
        tg[j] = tg[j] + rt[j].astype(F32)
        ref = ref_t[j]
        return (
            jnp.maximum(top_m, jnp.max(logits[0:256], 0, keepdims=True)),
            jnp.maximum(top_t, jnp.max(logits[256:384], 0, keepdims=True)),
            jnp.maximum(ref_m, jnp.max(ref[0:256], 0, keepdims=True)),
            jnp.maximum(ref_tl, jnp.max(ref[256:384], 0, keepdims=True)),
        )

    top_m, top_t, ref_m, ref_tl = lax.fori_loop(0, 4, maxima, (lowest,) * 4)
    top_t = jnp.maximum(top_t, swap_halves(top_t))
    ref_tl = jnp.maximum(ref_tl, swap_halves(ref_tl))

    row = lax.broadcasted_iota(jnp.int32, (256, 128), 0)
    main_col = jnp.where(row < 128, row, row + 384)
    tail_row = lax.broadcasted_iota(jnp.int32, (128, 128), 0)
    tail_col = jnp.where(low128, tail_row, tail_row + 512)
    wanted = act_ref[...] - v * 1024
    wanted_m = wanted[:, 0:128]
    wanted_t = jnp.concatenate([wanted[:, 128:192]] * 2, axis=1)

    def sums(j, carry):
        def part(logits, tangent, ref, top, ref_top, col, wanted, old):
            weights = jnp.exp(logits - top)
            ref_weights = jnp.exp(ref - ref_top)
            picked = jnp.where(col + j * 128 == wanted, logits, 0.0)
            new = (weights, weights * tangent, ref_weights, ref_weights * (ref - logits), picked)
            return tuple(o + jnp.sum(n, 0, keepdims=True) for o, n in zip(old, new))

        main = part(lg[j, 0:256], tg[j, 0:256], ref_t[j, 0:256], top_m, ref_m, main_col, wanted_m, carry[0:5])
        tail = part(
            lg[j, 256:384], tg[j, 256:384], ref_t[j, 256:384], top_t, ref_tl, tail_col, wanted_t, carry[5:10]
        )
        return main + tail

    found = lax.fori_loop(0, 4, sums, (jnp.zeros((1, 128), F32),) * 10)
    tails = [value + swap_halves(value) for value in found[5:10]]
    rows_m = [top_m, found[0], found[1], ref_m, found[2], found[3], found[4]]
    rows_t = [top_t, tails[0], tails[1], ref_tl, tails[2], tails[3], tails[4]]
    for i in range(7):
        sst[0, i : i + 1, 0:128] = rows_m[i]
        sst[0, i : i + 1, 128:256] = rows_t[i]
    sst[:, 7:8] = jnp.zeros((2, 1, 256), F32)

    now = [send(sst.at[0], sbuf.at[i], c_s.at[i], c_r.at[i], at_xy(*plane[i])) for i in range(15)]
    for copy in now:
        copy.start()
    for copy in now:
        copy.wait_recv()
    merged = merge([sst[0]] + [sbuf[i] for i in range(15)])
    for i in range(7):
        sst[1, i : i + 1] = merged[i]
    now = [send(sst.at[1], sbuf.at[i], c_s.at[i], c_r.at[i], at_z(0, i - 14)) for i in range(15, 18)]
    for copy in now:
        copy.start()
    for copy in now:
        copy.wait_recv()
    merged = merge([sst[1]] + [sbuf[i] for i in range(15, 18)])

    top, total, moment, ref_top, ref_sum, cross, chosen = merged
    log_total = top + jnp.log(total)
    mean_tangent = moment / total
    valid = val_ref[...].astype(F32)
    valid = jnp.concatenate([valid, valid[:, 128:192]], axis=1)
    penalty = valid * (cross / ref_sum - (ref_top + jnp.log(ref_sum)) + log_total)
    pen_ref[...] = penalty[:, 0:192]
    alp_ref[...] = (chosen - log_total)[:, 0:192]
    leaving = [
        pltpu.make_async_copy(pen_ref, pen_hbm, out_sem.at[3]),
        pltpu.make_async_copy(alp_ref, alp_hbm, out_sem.at[4]),
    ]
    for copy in leaving:
        copy.start()

    def d_sibling(j):
        return raw(fbuf.at[0, j], fbuf.at[1, j], d1_s.at[j], d1_r.at[j], sibling)

    def d_across(j):
        return raw(fbuf.at[0, j], fbuf.at[2, j], d2_s.at[j], d2_r.at[j], across)

    def d_relay(j):
        return raw(fbuf.at[2, j], fbuf.at[3, j], d3_s.at[j], d3_r.at[j], sibling)

    @pl.loop(0, 4)
    def _(j):
        def part(rows, lanes):
            return (
                valid[:, lanes] * jnp.exp(lg[j, rows] - log_total[:, lanes]) * (tg[j, rows] - mean_tangent[:, lanes])
            ).astype(BF16)

        fbuf[0, j, 0:256] = part(slice(0, 256), slice(0, 128))
        fbuf[0, j, 256:384] = part(slice(256, 384), slice(128, 256))
        d_across(j).start()
        d_sibling(j).start()

    def unpack_fisher(r):
        for j in range(4):
            block = fbuf[r, j]
            tail = block[256:384]
            zero = jnp.zeros_like(tail)
            for half in range(2):
                rows = slice(half * 512 + j * 128, half * 512 + j * 128 + 128)
                fun[rows, r * 256 : r * 256 + 128] = block[half * 128 : half * 128 + 128]
                fun[rows, r * 256 + 128 : r * 256 + 256] = (
                    jnp.where(low128, tail, zero) if half == 0 else jnp.where(low128, zero, tail)
                )

    low192 = low_lanes(192)

    def hidden_part(p):
        @pl.loop(0, 4)
        def _(k):
            rows = pl.ds(pl.multiple_of(k * 192, 192), 192)
            part = jnp.dot(head_ref[rows, :], fun[:, p * 512 : p * 512 + 512], preferred_element_type=F32)
            even, odd = part[:, 128:256], part[:, 384:512]
            tail = jnp.where(low192, even + swap_halves(even), odd + swap_halves(odd))
            ep[p, k, :, :, 0:128] = part[:, 0:128].reshape(4, 48, 128)
            ep[p, k, :, :, 128:256] = part[:, 256:384].reshape(4, 48, 128)
            ep[p, k, :, :, 256:384] = tail.reshape(4, 48, 128)

    e1, e2 = {}, {}
    for p in range(2):
        for side, d in ((0, 1), (1, 3)):
            e1[p, side] = send(e1s.at[p, side], e1r.at[p, side], e1_s.at[p, side], e1_q.at[p, side], at_x(d))
            e2[p, side] = send(e2s.at[p, side], e2r.at[p, side], e2_s.at[p, side], e2_q.at[p, side], at_x(d))

    def e_first(p):
        far = (x + 2) % 4
        e1s[p, 0] = ep[p, 0:2, far].astype(BF16)
        e1s[p, 1] = ep[p, 2:4, far].astype(BF16)
        e1[p, 0].start()
        e1[p, 1].start()

    def e_second(p):
        e2s[p, 0, 2:4] = ep[p, 2:4, right_x].astype(BF16)
        e2s[p, 1, 0:2] = ep[p, 0:2, left_x].astype(BF16)
        e1[p, 0].wait_recv()
        e2s[p, 0, 0:2] = (ep[p, 0:2, right_x] + e1r[p, 0].astype(F32)).astype(BF16)
        e2[p, 0].start()
        e1[p, 1].wait_recv()
        e2s[p, 1, 2:4] = (ep[p, 2:4, left_x] + e1r[p, 1].astype(F32)).astype(BF16)
        e2[p, 1].start()

    ez = {
        (r, d): send(
            zsend.at[r, (zh + d) % 4], zrecv.at[r, d], ez_s.at[r * 4 + d], ez_r.at[r * 4 + d], at_z(r, d)
        )
        for r, d in column
    }

    def e_third(p):
        e2[p, 0].wait_recv()
        e2[p, 1].wait_recv()
        total_x = (ep[p, :, x] + e2r[p, 0].astype(F32) + e2r[p, 1].astype(F32)).astype(BF16)
        for odd in range(2):
            zsend[p * 2 + odd, :, :, 0:128] = total_x[:, :, odd * 128 : odd * 128 + 128]
            zsend[p * 2 + odd, :, :, 128:256] = total_x[:, :, 256:384]
        for r in (p * 2 + 1, p * 2):
            for d in range(4):
                if (r, d) != (0, 0):
                    ez[r, d].start()

    loops += [d_across, d_sibling]
    unpack_fisher(0)
    for j in range(4):
        d_sibling(j).wait_recv()
    unpack_fisher(1)
    for j in range(2):
        d_across(j).wait_recv()
        d_relay(j).start()
    hidden_part(0)
    e_first(0)
    for j in range(2, 4):
        d_across(j).wait_recv()
        d_relay(j).start()
    loops.append(d_relay)
    e_second(0)
    unpack_fisher(2)
    for j in range(4):
        d_relay(j).wait_recv()
    unpack_fisher(3)
    hidden_part(1)
    e_first(1)

    def product(k):
        rows = slice(k * 256, k * 256 + 256)
        return pltpu.make_async_copy(hp_ref.at[rows], hp_hbm.at[rows], out_sem.at[k])

    def head_part(k):
        rows = slice(k * 256, k * 256 + 256)

        @pl.loop(0, 2)
        def _(n):
            cols = pl.ds(pl.multiple_of(n * 512, 512), 512)
            hp_ref[rows, cols] = lax.dot_general(
                hun[rows, :], fun[cols, :], (((1,), (1,)), ((), ())), preferred_element_type=F32
            ).astype(BF16)

        product(k).start()

    e_third(0)
    head_part(0)
    e_second(1)
    head_part(1)
    e_third(1)
    head_part(2)
    for r in ORDER:
        parts = []
        for d in range(4):
            if (r, d) != (0, 0):
                ez[r, d].wait_recv()
                parts.append(zrecv[r, d].astype(F32))
            else:
                parts.append(zsend[0, zh].astype(F32))
        whole = sum(parts)
        place = tok_of(r)
        tail = swap_halves(whole[:, 128:256]) if r % 2 else whole[:, 128:256]
        ysum[place, :, 0:128] = whole[:, 0:128]
        ysum[place, :, 128:256] = tail
        ysend[place, :, 0:128] = whole[:, 0:128].astype(BF16)
        ysend[place, :, 128:256] = tail.astype(BF16)
    ey = [
        send(ysend.at[(y + d + 1) % 4], yrecv.at[d], ey_s.at[d], ey_r.at[d], at_y(d + 1)) for d in range(3)
    ]
    for copy in ey:
        copy.start()
    for copy in ey:
        copy.wait_recv()
    total_y = ysum[y] + sum(yrecv[d].astype(F32) for d in range(3))
    hid_ref[...] = total_y[:, 0:192].astype(BF16)
    leaving.append(pltpu.make_async_copy(hid_ref, hid_hbm, out_sem.at[5]))
    leaving[2].start()
    finish()
    for copy in leaving + [product(k) for k in range(3)]:
        copy.wait()


def copy_out(*refs):
    held, in_sem, out_sem = refs[8:12], refs[12], refs[13]
    views = []
    for k in range(4):
        rows = slice(k * 192, k * 192 + 192)
        views.append((refs[0].at[rows], held[0].at[rows], refs[4].at[rows]))
    views += [(refs[i], held[i], refs[4 + i]) for i in range(1, 4)]
    loads = [pltpu.make_async_copy(a, b, in_sem.at[i]) for i, (a, b, _) in enumerate(views)]
    stores = [pltpu.make_async_copy(b, c, out_sem.at[i]) for i, (_, b, c) in enumerate(views)]
    for load in loads:
        load.start()
    for load, store in zip(loads, stores):
        load.wait()
        store.start()
    for store in stores:
        store.wait()


def body(hidden, hidden_tangent, head, head_tangent, ref_logits, actions, valid):
    vm, dma = pltpu.VMEM, pltpu.SemaphoreType.DMA
    hbm = pl.BlockSpec(memory_space=pl.ANY)
    shapes = (
        jax.ShapeDtypeStruct((768, 1024), BF16),
        jax.ShapeDtypeStruct((48, 192), BF16),
        jax.ShapeDtypeStruct((1, 192), F32),
        jax.ShapeDtypeStruct((1, 192), F32),
    )
    results = pl.pallas_call(
        kernel,
        out_shape=shapes,
        in_specs=[hbm] * 7,
        out_specs=(hbm,) * 4,
        scratch_shapes=[
            vm((48, 192), BF16),
            vm((48, 192), BF16),
            vm((1, 192), jnp.int32),
            vm((1, 192), jnp.int32),
            vm((48, 192), BF16),
            vm((1, 192), F32),
            vm((1, 192), F32),
            vm((768, 1024), BF16),
            vm((768, 1024), BF16),
            vm((192, 1024), BF16),
            vm((768, 1024), BF16),
            vm((4, 256, 768), BF16),
            vm((4, 256, 768), BF16),
            vm((4, 384, 128), F32),
            vm((48, 384), BF16),
            vm((4, 4, 4, 48, 384), BF16),
            vm((768, 1024), BF16),
            vm((768, 256), BF16),
            vm((4, 2, 384, 128), F32),
            vm((4, 2, 384, 128), F32),
            vm((4, 2, 384, 128), F32),
            vm((4, 2, 384, 128), F32),
            vm((4, 384, 128), F32),
            vm((4, 384, 128), BF16),
            vm((4, 384, 128), F32),
            vm((4, 384, 128), BF16),
            vm((4, 384, 128), F32),
            vm((4, 384, 128), F32),
            vm((2, 8, 256), F32),
            vm((18, 8, 256), F32),
            vm((4, 4, 384, 128), BF16),
            vm((1024, 1024), BF16),
            vm((2, 4, 4, 48, 384), F32),
            vm((2, 2, 2, 48, 384), BF16),
            vm((2, 2, 2, 48, 384), BF16),
            vm((2, 2, 4, 48, 384), BF16),
            vm((2, 2, 4, 48, 384), BF16),
            vm((4, 4, 48, 256), BF16),
            vm((4, 4, 48, 256), BF16),
            vm((4, 48, 256), BF16),
            vm((3, 48, 256), BF16),
            vm((4, 48, 256), F32),
            dma((7,)), dma((6,)),
            dma((4, 4)), dma((4, 4)),
            dma((4,)), dma((16,)),
            dma((4, 4)), dma((4, 4)),
            dma((4,)), dma((4,)), dma((4,)), dma((4,)),
            dma((4,)), dma((4,)), dma((4,)), dma((4,)),
            dma((18,)), dma((18,)),
            dma((4,)), dma((4,)), dma((4,)), dma((4,)), dma((4,)), dma((4,)),
            dma((2, 2)), dma((2, 2)), dma((2, 2)), dma((2, 2)),
            dma((16,)), dma((16,)),
            dma((3,)), dma((3,)),
        ],
        compiler_params=pltpu.CompilerParams(
            collective_id=0, has_side_effects=True, vmem_limit_bytes=56 * 1024 * 1024
        ),
    )(hidden.T, hidden_tangent.T, head, head_tangent, ref_logits, actions[None, :], valid[None, :])
    head_product, hid, penalty, logprob = pl.pallas_call(
        copy_out,
        out_shape=shapes,
        in_specs=[hbm] * 4,
        out_specs=(hbm,) * 4,
        scratch_shapes=[vm(shape.shape, shape.dtype) for shape in shapes] + [dma((7,)), dma((7,))],
    )(*results)
    return (head_product, hid.T, penalty.reshape(192), logprob.reshape(192))


def solution(mesh):
    return jax.shard_map(
        body,
        mesh=mesh,
        in_specs=(P("tok", "vocab"),) * 5 + (P("tok"), P("tok")),
        out_specs=(P("tok", "vocab"), P("tok", "vocab"), P("tok"), P("tok")),
        check_vma=False,
    )
```

```python
import functools

import jax
import jax.numpy as jnp
from jax import lax
from jax.experimental import pallas as pl
from jax.experimental.pallas import tpu as pltpu
from jax.sharding import PartitionSpec as P

F32 = jnp.float32
BF16 = jnp.bfloat16
MESH = pl.DeviceIdType.MESH
ORDER = (3, 2, 1, 0)


def low_lanes(rows):
    return lax.broadcasted_iota(jnp.int32, (rows, 128), 1) < 64


def swap_halves(value):
    return pltpu.roll(value, 64, 1)


def merge(stats):
    tops = [s[0:1] for s in stats]
    ref_tops = [s[3:4] for s in stats]
    top = functools.reduce(jnp.maximum, tops)
    ref_top = functools.reduce(jnp.maximum, ref_tops)
    scale = [jnp.exp(a - top) for a in tops]
    ref_scale = [jnp.exp(a - ref_top) for a in ref_tops]
    n = range(len(stats))
    return (
        top,
        sum(stats[i][1:2] * scale[i] for i in n),
        sum(stats[i][2:3] * scale[i] for i in n),
        ref_top,
        sum(stats[i][4:5] * ref_scale[i] for i in n),
        sum(stats[i][5:6] * ref_scale[i] for i in n),
        sum(stats[i][6:7] for i in n),
    )


class Sent:
    def __init__(self, book, copy):
        self.book, self.copy, self.got = book, copy, False

    def start(self):
        self.copy.start()
        self.book.append(self)

    def wait_recv(self):
        self.copy.wait_recv()
        self.got = True

    def wait_send(self):
        self.copy.wait_send()


def kernel(
    h_hbm, g_hbm, head_hbm, ht_hbm, ref_hbm, act_hbm, val_hbm,
    hp_hbm, hid_hbm, pen_hbm, alp_hbm,
    h_ref, g_ref, act_ref, val_ref, hid_ref, pen_ref, alp_ref,
    head_ref, ht_ref, ref_ref, hp_ref,
    head_t, ht_t, ref_t, sbk, hbuf, hun, tun,
    out3, in3, out1, in1, xl, xt, rl, rt, lg, tg,
    sst, sbuf, fbuf, fun, ep,
    e1s, e1r, e2s, e2r, zsend, zrecv, ysend, yrecv, ysum,
    in_sem, out_sem,
    ya_s, ya_r, za_s, za_r, xa_s, xa_r, b3_s, b3_r, b1_s, b1_r, bl_s, bl_r, bt_s, bt_r,
    c_s, c_r, d1_s, d1_r, d2_s, d2_r, d3_s, d3_r, e1_s, e1_q, e2_s, e2_q, ez_s, ez_r, ey_s, ey_r,
):
    loads = [
        pltpu.make_async_copy(src, dst, in_sem.at[i])
        for i, (src, dst) in enumerate(
            (
                (h_hbm, h_ref), (g_hbm, g_ref), (head_hbm, head_ref), (ht_hbm, ht_ref),
                (ref_hbm, ref_ref), (act_hbm, act_ref), (val_hbm, val_ref),
            )
        )
    ]
    for load in loads:
        load.start()
    v = lax.axis_index("vocab")
    t = lax.axis_index("tok")
    y, zh, x = lax.div(v, 16), lax.rem(lax.div(v, 4), 4), lax.rem(v, 4)
    zl, c = lax.div(t, 2), lax.rem(t, 2)
    xs, ys, zs = ([place] + [lax.rem(place + d, 4) for d in (1, 2, 3)] for place in (x, y, zh))
    y_base, z_base = [place * 16 for place in ys], [place * 4 for place in zs]
    rest_x, rest_z, rest_y = v - x, v - z_base[0], v - y_base[0]
    toks = [z + core for z in (2 * zl, 2 - 2 * zl) for core in (c, 1 - c)]
    x_base = [rest_x - y_base[0] + place for place in xs]

    def at_x(d):
        return (rest_x + xs[d], t)

    def at_xy(dx, dy):
        return (y_base[dy] + x_base[dx], t)

    def at_y(d):
        return (rest_y + y_base[d], t)

    def tok_of(r):
        return toks[r]

    def at_z(r, d):
        return (rest_z + z_base[d], toks[r])

    sent, loops = [], []

    def send(src, dst, ssem, rsem, device):
        return Sent(
            sent,
            pltpu.make_async_remote_copy(
                src_ref=src, dst_ref=dst, send_sem=ssem, recv_sem=rsem,
                device_id=device, device_id_type=MESH,
            ),
        )

    def raw(src, dst, ssem, rsem, device):
        return send(src, dst, ssem, rsem, device).copy

    def finish():
        zy_finish()
        for copy in sent:
            copy.wait_send()
        if loops:

            @pl.loop(0, 4)
            def _(j):
                for copy_of in loops:
                    copy_of(j).wait_send()

    barrier = pltpu.get_barrier_semaphore()
    column = [(r, d) for r in ORDER for d in range(4) if (r, d) != (0, 0)]
    plane = [(dx, dy) for dx in range(4) for dy in range(4) if (dx, dy) != (0, 0)]
    peers = [at_xy(dx, dy) for dx, dy in plane] + [at_z(r, d) for r, d in column]
    for peer in peers:
        pl.semaphore_signal(barrier, inc=1, device_id=peer, device_id_type=MESH)
    for load in loads:
        load.wait()
    h, g = h_ref[...].astype(F32), g_ref[...].astype(F32)
    sbk[:, 0:128] = h[:, 0:128].astype(BF16)
    sbk[:, 128:256] = g[:, 0:128].astype(BF16)
    sbk[:, 256:384] = jnp.concatenate([h[:, 128:192], g[:, 128:192]], axis=1).astype(BF16)

    def turn(src, dst, j):
        for half in range(2):
            cols = slice(half * 512 + j * 128, half * 512 + j * 128 + 128)
            dst[j, half * 128 : half * 128 + 128] = src[:, cols].T

    def turn_ref(j):
        a, b = slice(j * 128, j * 128 + 128), slice(512 + j * 128, 512 + j * 128 + 128)
        ref_t[j, 0:128] = ref_ref[0:128, a].astype(F32).T
        ref_t[j, 128:256] = ref_ref[0:128, b].astype(F32).T
        tails = jnp.concatenate([ref_ref[128:192, a].astype(F32), ref_ref[128:192, b].astype(F32)], axis=0)
        ref_t[j, 256:384] = tails.T

    turn(head_ref, head_t, 0)
    turn(head_ref, head_t, 1)
    turn(head_ref, head_t, 2)
    turn(head_ref, head_t, 3)
    turn(ht_ref, ht_t, 0)

    pl.semaphore_wait(barrier, len(peers))

    slot = lax.rem(zl + lax.div(y, 2), 2) * 2 + lax.rem(c + y, 2)

    def z_copy(d):
        device = (rest_z + z_base[d], y)
        return raw(sbk, hbuf.at[slot, zh, x], za_s.at[d], za_r.at[slot * 4 + d], device)

    def z_wait(r, d):
        into = hbuf.at[r, zs[(4 - d) % 4], x]
        raw(sbk, into, za_s.at[d], za_r.at[r * 4 + d], at_z(r, 1)).wait_recv()

    for d in (1, 2, 3):
        z_copy(d).start()

    @pl.when(t != y)
    def _():
        z_copy(0).start()

    @pl.when(t == y)
    def _():
        hbuf[0, zh, x] = sbk[...]

    away = lax.rem(y + 4 - t, 4)

    def y_copy(r, k):
        part = hbuf.at[r, :, x] if k < 2 else hbuf.at[r, (k - 2) * 2 : (k - 2) * 2 + 2, x]
        return raw(part, part, ya_s.at[r, k], ya_r.at[r, k], at_y(3 if k % 2 else 1))

    def y_stage(r):
        @pl.when(away == 0)
        def _():
            for d in range(4):
                if (r, d) != (0, 0):
                    z_wait(r, d)
            y_copy(r, 0).start()
            y_copy(r, 1).start()

        @pl.when(away == 1)
        def _():
            y_copy(r, 0).wait_recv()
            y_copy(r, 2).start()

        @pl.when(away == 3)
        def _():
            y_copy(r, 1).wait_recv()
            y_copy(r, 3).start()

        @pl.when(away == 2)
        def _():
            y_copy(r, 2).wait_recv()
            y_copy(r, 3).wait_recv()

    def zy_finish():
        for d in (1, 2, 3):
            z_copy(d).wait_send()

        @pl.when(t != y)
        def _():
            z_copy(0).wait_send()

        for role, kinds in ((0, (0, 1)), (1, (2,)), (3, (3,))):

            @pl.when(away == role)
            def _():
                for r in range(4):
                    for k in kinds:
                        y_copy(r, k).wait_send()

    left_x, right_x = xs[3], xs[1]
    x_first, x_second = {}, {}
    for r in ORDER:
        own = hbuf.at[r, :, x]
        x_first[r] = (
            send(own, own, xa_s.at[r, 0], xa_r.at[r, 0], at_x(1)),
            send(own, own, xa_s.at[r, 1], xa_r.at[r, 1], at_x(3)),
        )
        from_left = hbuf.at[r, 0:2, left_x]
        from_right = hbuf.at[r, 2:4, right_x]
        x_second[r] = (
            send(from_left, from_left, xa_s.at[r, 2], xa_r.at[r, 2], at_x(1)),
            send(from_right, from_right, xa_s.at[r, 3], xa_r.at[r, 3], at_x(3)),
        )

    def x_start(r):
        y_stage(r)
        for copy in x_first[r]:
            copy.start()

    def x_forward(r):
        for first, second in zip(x_first[r], x_second[r]):
            first.wait_recv()
            second.start()

    def unpack(r):
        for copy in x_second[r]:
            copy.wait_recv()
        low = low_lanes(768)
        block = hbuf[r].reshape(768, 384)
        tails = block[:, 256:384].astype(F32)
        other = swap_halves(tails)
        hun[:, r * 256 : r * 256 + 128] = block[:, 0:128]
        hun[:, r * 256 + 128 : r * 256 + 256] = jnp.where(low, tails, other).astype(BF16)
        tun[:, 0:128] = block[:, 128:256]
        tun[:, 128:256] = jnp.where(low, other, tails).astype(BF16)

    low128 = low_lanes(128)

    def pack(value):
        tail = jnp.where(low128, value[0:128, 128:256], value[128:256, 128:256])
        return value[:, 0:128], tail

    def partial(r, j):
        h = hun[:, r * 256 : r * 256 + 256]
        logits = jnp.dot(head_t[j], h, preferred_element_type=F32)
        tangent = jnp.dot(head_t[j], tun[...], preferred_element_type=F32) + jnp.dot(
            ht_t[j], h, preferred_element_type=F32
        )
        return pack(logits) + pack(tangent)

    sibling = (v, tok_of(1))
    across = (v, tok_of(2))

    def to_sibling(j, out, into, ssem, rsem):
        return raw(out.at[j], into.at[j], ssem.at[j], rsem.at[j], sibling)

    def cross_l(j):
        return raw(xl.at[j], rl.at[j], bl_s.at[j], bl_r.at[j], across)

    def cross_t(j):
        return raw(xt.at[j], rt.at[j], bt_s.at[j], bt_r.at[j], across)

    def give(r, out, into, ssem, rsem):
        @pl.loop(0, 4)
        def _(j):
            lm, lt, tm, tt = partial(r, j)
            out[j, 0, 0:256] = lm
            out[j, 0, 256:384] = lt
            out[j, 1, 0:256] = tm
            out[j, 1, 256:384] = tt
            to_sibling(j, out, into, ssem, rsem).start()

    turn(ht_ref, ht_t, 1)
    x_start(3)
    turn(ht_ref, ht_t, 2)
    x_start(2)
    x_forward(3)
    x_forward(2)
    turn(ht_ref, ht_t, 3)
    unpack(3)
    give(3, out3, in3, b3_s, b3_r)
    loops.append(lambda j: to_sibling(j, out3, in3, b3_s, b3_r))
    unpack(2)

    @pl.loop(0, 4)
    def _(j):
        lm, lt, tm, tt = partial(2, j)
        to_sibling(j, out3, in3, b3_s, b3_r).wait_recv()
        xl[j, 0:256] = lm + in3[j, 0, 0:256]
        xl[j, 256:384] = lt + in3[j, 0, 256:384]
        xt[j, 0:256] = (tm + in3[j, 1, 0:256]).astype(BF16)
        xt[j, 256:384] = (tt + in3[j, 1, 256:384]).astype(BF16)
        cross_l(j).start()
        cross_t(j).start()

    loops += [cross_l, cross_t]
    x_start(1)
    x_start(0)
    x_forward(1)
    for j in range(4):
        turn_ref(j)
    x_forward(0)
    unpack(1)
    give(1, out1, in1, b1_s, b1_r)
    loops.append(lambda j: to_sibling(j, out1, in1, b1_s, b1_r))
    unpack(0)

    @pl.loop(0, 4)
    def _(j):
        lm, lt, tm, tt = partial(0, j)
        to_sibling(j, out1, in1, b1_s, b1_r).wait_recv()
        lg[j, 0:256] = lm + in1[j, 0, 0:256]
        lg[j, 256:384] = lt + in1[j, 0, 256:384]
        tg[j, 0:256] = tm + in1[j, 1, 0:256]
        tg[j, 256:384] = tt + in1[j, 1, 256:384]

    lowest = jnp.full((1, 128), -jnp.inf, F32)

    def maxima(j, carry):
        top_m, top_t, ref_m, ref_tl = carry
        cross_l(j).wait_recv()
        cross_t(j).wait_recv()
        logits = lg[j] + rl[j]
        lg[j] = logits
        tg[j] = tg[j] + rt[j].astype(F32)
        ref = ref_t[j]
        return (
            jnp.maximum(top_m, jnp.max(logits[0:256], 0, keepdims=True)),
            jnp.maximum(top_t, jnp.max(logits[256:384], 0, keepdims=True)),
            jnp.maximum(ref_m, jnp.max(ref[0:256], 0, keepdims=True)),
            jnp.maximum(ref_tl, jnp.max(ref[256:384], 0, keepdims=True)),
        )

    top_m, top_t, ref_m, ref_tl = lax.fori_loop(0, 4, maxima, (lowest,) * 4)
    top_t = jnp.maximum(top_t, swap_halves(top_t))
    ref_tl = jnp.maximum(ref_tl, swap_halves(ref_tl))

    row = lax.broadcasted_iota(jnp.int32, (256, 128), 0)
    main_col = jnp.where(row < 128, row, row + 384)
    tail_row = lax.broadcasted_iota(jnp.int32, (128, 128), 0)
    tail_col = jnp.where(low128, tail_row, tail_row + 512)
    wanted = act_ref[...] - v * 1024
    wanted_m = wanted[:, 0:128]
    wanted_t = jnp.concatenate([wanted[:, 128:192]] * 2, axis=1)

    def sums(j, carry):
        def part(logits, tangent, ref, top, ref_top, col, wanted, old):
            weights = jnp.exp(logits - top)
            ref_weights = jnp.exp(ref - ref_top)
            picked = jnp.where(col + j * 128 == wanted, logits, 0.0)
            new = (weights, weights * tangent, ref_weights, ref_weights * (ref - logits), picked)
            return tuple(o + jnp.sum(n, 0, keepdims=True) for o, n in zip(old, new))

        main = part(lg[j, 0:256], tg[j, 0:256], ref_t[j, 0:256], top_m, ref_m, main_col, wanted_m, carry[0:5])
        tail = part(
            lg[j, 256:384], tg[j, 256:384], ref_t[j, 256:384], top_t, ref_tl, tail_col, wanted_t, carry[5:10]
        )
        return main + tail

    found = lax.fori_loop(0, 4, sums, (jnp.zeros((1, 128), F32),) * 10)
    tails = [value + swap_halves(value) for value in found[5:10]]
    rows_m = [top_m, found[0], found[1], ref_m, found[2], found[3], found[4]]
    rows_t = [top_t, tails[0], tails[1], ref_tl, tails[2], tails[3], tails[4]]
    for i in range(7):
        sst[0, i : i + 1, 0:128] = rows_m[i]
        sst[0, i : i + 1, 128:256] = rows_t[i]
    sst[:, 7:8] = jnp.zeros((2, 1, 256), F32)

    now = [send(sst.at[0], sbuf.at[i], c_s.at[i], c_r.at[i], at_xy(*plane[i])) for i in range(15)]
    for copy in now:
        copy.start()
    for copy in now:
        copy.wait_recv()
    merged = merge([sst[0]] + [sbuf[i] for i in range(15)])
    for i in range(7):
        sst[1, i : i + 1] = merged[i]
    now = [send(sst.at[1], sbuf.at[i], c_s.at[i], c_r.at[i], at_z(0, i - 14)) for i in range(15, 18)]
    for copy in now:
        copy.start()
    for copy in now:
        copy.wait_recv()
    merged = merge([sst[1]] + [sbuf[i] for i in range(15, 18)])

    top, total, moment, ref_top, ref_sum, cross, chosen = merged
    log_total = top + jnp.log(total)
    mean_tangent = moment / total
    valid = val_ref[...].astype(F32)
    valid = jnp.concatenate([valid, valid[:, 128:192]], axis=1)
    penalty = valid * (cross / ref_sum - (ref_top + jnp.log(ref_sum)) + log_total)
    pen_ref[...] = penalty[:, 0:192]
    alp_ref[...] = (chosen - log_total)[:, 0:192]
    leaving = [
        pltpu.make_async_copy(pen_ref, pen_hbm, out_sem.at[3]),
        pltpu.make_async_copy(alp_ref, alp_hbm, out_sem.at[4]),
    ]
    for copy in leaving:
        copy.start()

    def d_sibling(j):
        return raw(fbuf.at[0, j], fbuf.at[1, j], d1_s.at[j], d1_r.at[j], sibling)

    def d_across(j):
        return raw(fbuf.at[0, j], fbuf.at[2, j], d2_s.at[j], d2_r.at[j], across)

    def d_relay(j):
        return raw(fbuf.at[2, j], fbuf.at[3, j], d3_s.at[j], d3_r.at[j], sibling)

    @pl.loop(0, 4)
    def _(j):
        def part(rows, lanes):
            return (
                valid[:, lanes] * jnp.exp(lg[j, rows] - log_total[:, lanes]) * (tg[j, rows] - mean_tangent[:, lanes])
            ).astype(BF16)

        fbuf[0, j, 0:256] = part(slice(0, 256), slice(0, 128))
        fbuf[0, j, 256:384] = part(slice(256, 384), slice(128, 256))
        d_across(j).start()
        d_sibling(j).start()

    def unpack_fisher(r):
        for j in range(4):
            block = fbuf[r, j]
            tail = block[256:384]
            zero = jnp.zeros_like(tail)
            for half in range(2):
                rows = slice(half * 512 + j * 128, half * 512 + j * 128 + 128)
                fun[rows, r * 256 : r * 256 + 128] = block[half * 128 : half * 128 + 128]
                fun[rows, r * 256 + 128 : r * 256 + 256] = (
                    jnp.where(low128, tail, zero) if half == 0 else jnp.where(low128, zero, tail)
                )

    low192 = low_lanes(192)

    def hidden_part(p):
        @pl.loop(0, 4)
        def _(k):
            rows = pl.ds(pl.multiple_of(k * 192, 192), 192)
            part = jnp.dot(head_ref[rows, :], fun[:, p * 512 : p * 512 + 512], preferred_element_type=F32)
            even, odd = part[:, 128:256], part[:, 384:512]
            tail = jnp.where(low192, even + swap_halves(even), odd + swap_halves(odd))
            ep[p, k, :, :, 0:128] = part[:, 0:128].reshape(4, 48, 128)
            ep[p, k, :, :, 128:256] = part[:, 256:384].reshape(4, 48, 128)
            ep[p, k, :, :, 256:384] = tail.reshape(4, 48, 128)

    e1, e2 = {}, {}
    for p in range(2):
        for side, d in ((0, 1), (1, 3)):
            e1[p, side] = send(e1s.at[p, side], e1r.at[p, side], e1_s.at[p, side], e1_q.at[p, side], at_x(d))
            e2[p, side] = send(e2s.at[p, side], e2r.at[p, side], e2_s.at[p, side], e2_q.at[p, side], at_x(d))

    def e_first(p):
        far = xs[2]
        e1s[p, 0] = ep[p, 0:2, far].astype(BF16)
        e1s[p, 1] = ep[p, 2:4, far].astype(BF16)
        e1[p, 0].start()
        e1[p, 1].start()

    def e_second(p):
        e2s[p, 0, 2:4] = ep[p, 2:4, right_x].astype(BF16)
        e2s[p, 1, 0:2] = ep[p, 0:2, left_x].astype(BF16)
        e1[p, 0].wait_recv()
        e2s[p, 0, 0:2] = (ep[p, 0:2, right_x] + e1r[p, 0].astype(F32)).astype(BF16)
        e2[p, 0].start()
        e1[p, 1].wait_recv()
        e2s[p, 1, 2:4] = (ep[p, 2:4, left_x] + e1r[p, 1].astype(F32)).astype(BF16)
        e2[p, 1].start()

    ez = {
        (r, d): send(
            zsend.at[r, zs[d]], zrecv.at[r, d], ez_s.at[r * 4 + d], ez_r.at[r * 4 + d], at_z(r, d)
        )
        for r, d in column
    }

    def e_third(p):
        e2[p, 0].wait_recv()
        e2[p, 1].wait_recv()
        total_x = (ep[p, :, x] + e2r[p, 0].astype(F32) + e2r[p, 1].astype(F32)).astype(BF16)
        for odd in range(2):
            zsend[p * 2 + odd, :, :, 0:128] = total_x[:, :, odd * 128 : odd * 128 + 128]
            zsend[p * 2 + odd, :, :, 128:256] = total_x[:, :, 256:384]
        for r in (p * 2 + 1, p * 2):
            for d in range(4):
                if (r, d) != (0, 0):
                    ez[r, d].start()

    loops += [d_across, d_sibling]
    unpack_fisher(0)
    for j in range(4):
        d_sibling(j).wait_recv()
    unpack_fisher(1)
    for j in range(2):
        d_across(j).wait_recv()
        d_relay(j).start()
    hidden_part(0)
    e_first(0)
    for j in range(2, 4):
        d_across(j).wait_recv()
        d_relay(j).start()
    loops.append(d_relay)
    e_second(0)
    unpack_fisher(2)
    for j in range(4):
        d_relay(j).wait_recv()
    unpack_fisher(3)
    hidden_part(1)
    e_first(1)

    def product(k):
        rows = slice(k * 256, k * 256 + 256)
        return pltpu.make_async_copy(hp_ref.at[rows], hp_hbm.at[rows], out_sem.at[k])

    def head_part(k):
        rows = slice(k * 256, k * 256 + 256)

        @pl.loop(0, 2)
        def _(n):
            cols = pl.ds(pl.multiple_of(n * 512, 512), 512)
            hp_ref[rows, cols] = lax.dot_general(
                hun[rows, :], fun[cols, :], (((1,), (1,)), ((), ())), preferred_element_type=F32
            ).astype(BF16)

        product(k).start()

    e_third(0)
    head_part(0)
    e_second(1)
    head_part(1)
    e_third(1)
    head_part(2)
    for r in ORDER:
        parts = []
        for d in range(4):
            if (r, d) != (0, 0):
                ez[r, d].wait_recv()
                parts.append(zrecv[r, d].astype(F32))
            else:
                parts.append(zsend[0, zh].astype(F32))
        whole = sum(parts)
        place = tok_of(r)
        tail = swap_halves(whole[:, 128:256]) if r % 2 else whole[:, 128:256]
        ysum[place, :, 0:128] = whole[:, 0:128]
        ysum[place, :, 128:256] = tail
        ysend[place, :, 0:128] = whole[:, 0:128].astype(BF16)
        ysend[place, :, 128:256] = tail.astype(BF16)
    ey = [
        send(ysend.at[ys[d + 1]], yrecv.at[d], ey_s.at[d], ey_r.at[d], at_y(d + 1)) for d in range(3)
    ]
    for copy in ey:
        copy.start()
    for copy in ey:
        copy.wait_recv()
    total_y = ysum[y] + sum(yrecv[d].astype(F32) for d in range(3))
    hid_ref[...] = total_y[:, 0:192].astype(BF16)
    leaving.append(pltpu.make_async_copy(hid_ref, hid_hbm, out_sem.at[5]))
    leaving[2].start()
    finish()
    for copy in leaving + [product(k) for k in range(3)]:
        copy.wait()


def copy_out(*refs):
    held, in_sem, out_sem = refs[8:12], refs[12], refs[13]
    views = []
    for k in range(4):
        rows = slice(k * 192, k * 192 + 192)
        views.append((refs[0].at[rows], held[0].at[rows], refs[4].at[rows]))
    views += [(refs[i], held[i], refs[4 + i]) for i in range(1, 4)]
    loads = [pltpu.make_async_copy(a, b, in_sem.at[i]) for i, (a, b, _) in enumerate(views)]
    stores = [pltpu.make_async_copy(b, c, out_sem.at[i]) for i, (_, b, c) in enumerate(views)]
    for load in loads:
        load.start()
    for load, store in zip(loads, stores):
        load.wait()
        store.start()
    for store in stores:
        store.wait()


def body(hidden, hidden_tangent, head, head_tangent, ref_logits, actions, valid):
    vm, dma = pltpu.VMEM, pltpu.SemaphoreType.DMA
    hbm = pl.BlockSpec(memory_space=pl.ANY)
    shapes = (
        jax.ShapeDtypeStruct((768, 1024), BF16),
        jax.ShapeDtypeStruct((48, 192), BF16),
        jax.ShapeDtypeStruct((1, 192), F32),
        jax.ShapeDtypeStruct((1, 192), F32),
    )
    results = pl.pallas_call(
        kernel,
        out_shape=shapes,
        in_specs=[hbm] * 7,
        out_specs=(hbm,) * 4,
        scratch_shapes=[
            vm((48, 192), BF16),
            vm((48, 192), BF16),
            vm((1, 192), jnp.int32),
            vm((1, 192), jnp.int32),
            vm((48, 192), BF16),
            vm((1, 192), F32),
            vm((1, 192), F32),
            vm((768, 1024), BF16),
            vm((768, 1024), BF16),
            vm((192, 1024), BF16),
            vm((768, 1024), BF16),
            vm((4, 256, 768), BF16),
            vm((4, 256, 768), BF16),
            vm((4, 384, 128), F32),
            vm((48, 384), BF16),
            vm((4, 4, 4, 48, 384), BF16),
            vm((768, 1024), BF16),
            vm((768, 256), BF16),
            vm((4, 2, 384, 128), F32),
            vm((4, 2, 384, 128), F32),
            vm((4, 2, 384, 128), F32),
            vm((4, 2, 384, 128), F32),
            vm((4, 384, 128), F32),
            vm((4, 384, 128), BF16),
            vm((4, 384, 128), F32),
            vm((4, 384, 128), BF16),
            vm((4, 384, 128), F32),
            vm((4, 384, 128), F32),
            vm((2, 8, 256), F32),
            vm((18, 8, 256), F32),
            vm((4, 4, 384, 128), BF16),
            vm((1024, 1024), BF16),
            vm((2, 4, 4, 48, 384), F32),
            vm((2, 2, 2, 48, 384), BF16),
            vm((2, 2, 2, 48, 384), BF16),
            vm((2, 2, 4, 48, 384), BF16),
            vm((2, 2, 4, 48, 384), BF16),
            vm((4, 4, 48, 256), BF16),
            vm((4, 4, 48, 256), BF16),
            vm((4, 48, 256), BF16),
            vm((3, 48, 256), BF16),
            vm((4, 48, 256), F32),
            dma((7,)), dma((6,)),
            dma((4, 4)), dma((4, 4)),
            dma((4,)), dma((16,)),
            dma((4, 4)), dma((4, 4)),
            dma((4,)), dma((4,)), dma((4,)), dma((4,)),
            dma((4,)), dma((4,)), dma((4,)), dma((4,)),
            dma((18,)), dma((18,)),
            dma((4,)), dma((4,)), dma((4,)), dma((4,)), dma((4,)), dma((4,)),
            dma((2, 2)), dma((2, 2)), dma((2, 2)), dma((2, 2)),
            dma((16,)), dma((16,)),
            dma((3,)), dma((3,)),
        ],
        compiler_params=pltpu.CompilerParams(
            collective_id=0, has_side_effects=True, vmem_limit_bytes=56 * 1024 * 1024
        ),
    )(hidden.T, hidden_tangent.T, head, head_tangent, ref_logits, actions[None, :], valid[None, :])
    head_product, hid, penalty, logprob = pl.pallas_call(
        copy_out,
        out_shape=shapes,
        in_specs=[hbm] * 4,
        out_specs=(hbm,) * 4,
        scratch_shapes=[vm(shape.shape, shape.dtype) for shape in shapes] + [dma((7,)), dma((7,))],
    )(*results)
    return (head_product, hid.T, penalty.reshape(192), logprob.reshape(192))


def solution(mesh):
    return jax.shard_map(
        body,
        mesh=mesh,
        in_specs=(P("tok", "vocab"),) * 5 + (P("tok"), P("tok")),
        out_specs=(P("tok", "vocab"), P("tok", "vocab"), P("tok"), P("tok")),
        check_vma=False,
    )
```
